256 devices in a mesh: ctx: 8 (over y, z_hi), dec: 8 (over z_lo, core), grp: 4 (over x).
Axes of the slice: x: 4, y: 4, z: 8 (z_hi: 2, z_lo: 4; z = z_hi * 4 + z_lo), core: 2. Of those that a mesh axis runs over, the one named last changes fastest.
Arguments:
- queries: bfloat16 [4, 128, 8192], P('grp', 'dec', 'ctx'), may hold values from -16 to 16
- prompt_kv: bfloat16 [4, 2, 32768, 2, 1024], P('grp', None, ('ctx', 'dec')), may hold values from -12 to 12
- suffix_kv: bfloat16 [4, 128, 256, 2, 1024], P('grp', 'dec', None, None, 'ctx'), may hold values from -18 to 18
- suffix_len: int32 [4, 128], P('grp', 'dec'), may hold values from 1 to 256, as said below
- group_of: int32 [4, 128], P('grp'), may hold values from 0 to 1, as said below
Outputs:
- attended: bfloat16 [4, 128, 8192], P('grp', 'dec', 'ctx')
The draws below stay inside these ranges and needn't reach their ends.
Inputs may be any that keep to these rules, and one draw needn't show every extreme that they name: `group_of`: in every block of 128 rows each value names exactly 64 rows. `suffix_len`: every block has a row of length 256.
All inputs are finite; a program needn't handle non-finite values.
Results may differ from the reference program's by a relative error of at most 0.012.
Values may be sent and summed in bfloat16 or wider, within the bound.
No kernel may reach another device: no remote copies, remote signals or barrier semaphores. Data moves between devices by JAX's collectives and lax.ppermute only.
A program may use at most 192 MiB of HBM per device.

```python
import jax
import jax.numpy as jnp
from jax import lax

H = 64
KVH = 8
HD = 128
G_DEV = 2
SUF = 256
SAMPLES = 64
ROWS = 128
PROMPT = 32768
N_GRP = 4


def draw_queries(key, part):
    key = jax.random.fold_in(key, 11)
    shape = (N_GRP, ROWS, H * HD)
    values = jnp.clip(jax.random.normal(key, shape, jnp.float32), -4.0, 4.0)
    return values.astype(jnp.bfloat16)


def draw_prompt_kv(key, part):
    key = jax.random.fold_in(key, 12)
    shape = (N_GRP, G_DEV, PROMPT, 2, KVH * HD)
    factor = jnp.array([3.0, 1.0], jnp.float32).reshape(1, 1, 1, 2, 1)
    values = jnp.clip(jax.random.normal(key, shape, jnp.float32), -4.0, 4.0) * factor
    return values.astype(jnp.bfloat16)


def draw_suffix_kv(key, part):
    key = jax.random.fold_in(key, 13)
    shape = (N_GRP, ROWS, SUF, 2, KVH * HD)
    factor = jnp.array([4.5, 1.0], jnp.float32).reshape(1, 1, 1, 2, 1)
    values = jnp.clip(jax.random.normal(key, shape, jnp.float32), -4.0, 4.0) * factor
    return values.astype(jnp.bfloat16)


def draw_suffix_len(key, part):
    key = jax.random.fold_in(key, 14)
    length_key, place_key = jax.random.split(key)
    lengths = jax.random.randint(length_key, (N_GRP, ROWS), 1, SUF + 1)
    longest = jax.random.randint(place_key, (N_GRP,), 0, ROWS)
    lengths = jnp.where(jnp.arange(ROWS)[None, :] == longest[:, None], SUF, lengths)
    return lengths.astype(jnp.int32)


def draw_group_of(key, part):
    key = jax.random.fold_in(key, 15)
    orders = jax.vmap(lambda block_key: jax.random.permutation(block_key, ROWS))(jax.random.split(key, N_GRP))
    return (orders // SAMPLES).astype(jnp.int32)


def setup_inputs(seed: int = 0) -> dict:
    seeds = jax.random.split(jax.random.key(seed), 6)
    queries = draw_queries(jax.random.fold_in(seeds[5], 71), 0)
    prompt_kv = draw_prompt_kv(jax.random.fold_in(seeds[5], 71), 0)
    suffix_kv = draw_suffix_kv(jax.random.fold_in(seeds[5], 71), 0)
    suffix_len = draw_suffix_len(jax.random.fold_in(seeds[5], 71), 0)
    group_of = draw_group_of(jax.random.fold_in(seeds[5], 71), 0)
    return dict(queries=queries, prompt_kv=prompt_kv, suffix_kv=suffix_kv, suffix_len=suffix_len, group_of=group_of)


def reference(queries, prompt_kv, suffix_kv, suffix_len, group_of):
    scale = HD ** -0.5
    repeat = H // KVH

    def one_block(items):
        query_rows, prompt, suffix, lengths, member_ids = items
        heads_q = query_rows.reshape(ROWS, KVH, repeat, HD)
        prompt_heads = prompt.reshape(G_DEV, PROMPT, 2, KVH, HD)
        suffix_heads = suffix.reshape(ROWS, SUF, 2, KVH, HD)
        member = member_ids[:, None] == jnp.arange(G_DEV, dtype=jnp.int32)[None, :]
        valid = jnp.arange(SUF, dtype=jnp.int32)[None, :] < lengths[:, None]

        def one_head(index):
            query_head = heads_q[:, index].astype(jnp.float32)
            keys_p = prompt_heads[:, :, 0, index].astype(jnp.float32)
            values_p = prompt_heads[:, :, 1, index].astype(jnp.float32)
            keys_s = suffix_heads[:, :, 0, index].astype(jnp.float32)
            values_s = suffix_heads[:, :, 1, index].astype(jnp.float32)
            scores_p = jnp.einsum("rhd,gpd->rghp", query_head, keys_p) * scale
            scores_s = jnp.einsum("rhd,rsd->rhs", query_head, keys_s) * scale
            chosen = member[:, :, None, None]
            keep = valid[:, None, :]
            peak_p = jnp.max(jnp.where(chosen, scores_p, -jnp.inf), axis=(1, 3))
            peak_s = jnp.max(jnp.where(keep, scores_s, -jnp.inf), axis=2)
            peak = jnp.maximum(peak_p, peak_s)
            probs_p = jnp.where(chosen, jnp.exp(scores_p - peak[:, None, :, None]), 0.0)
            probs_s = jnp.where(keep, jnp.exp(scores_s - peak[:, :, None]), 0.0)
            totals = jnp.sum(probs_p, axis=(1, 3)) + jnp.sum(probs_s, axis=2)
            weights_p = lax.optimization_barrier(probs_p.astype(jnp.bfloat16)).astype(jnp.float32)
            weights_s = lax.optimization_barrier(probs_s.astype(jnp.bfloat16)).astype(jnp.float32)
            numerator = jnp.einsum("rghp,gpd->rhd", weights_p, values_p) + jnp.einsum("rhs,rsd->rhd", weights_s, values_s)
            return numerator / totals[:, :, None]

        outs = lax.map(one_head, jnp.arange(KVH, dtype=jnp.int32))
        return jnp.transpose(outs, (1, 0, 2, 3)).reshape(ROWS, H * HD).astype(jnp.bfloat16)

    return lax.map(one_block, (queries, prompt_kv, suffix_kv, suffix_len, group_of))
```

```python
import functools
import math

import jax
import jax.numpy as jnp
import numpy as np
from jax import lax
from jax.experimental import pallas as pl
from jax.experimental.pallas import tpu as pltpu
from jax.sharding import Mesh
from jax.sharding import PartitionSpec as P

HD = 128
REP = 8
C2 = HD ** (-0.5) * math.log2(math.e)
BIG = 1e30
F32 = jnp.float32
BF16 = jnp.bfloat16


def _dot_t(a, b):
    return lax.dot_general(a, b, (((1,), (1,)), ((), ())), preferred_element_type=F32)


def _pack(l2):
    hi = l2.astype(BF16).astype(F32)
    rest = l2 - hi
    mid = rest.astype(BF16).astype(F32)
    return hi, mid, rest - mid


def _stats(l2):
    lane = lax.broadcasted_iota(jnp.int32, l2.shape, 1)
    hi, mid, lo = _pack(jnp.where(lane < REP, l2, 0.0))
    return (hi + pltpu.roll(mid, REP, 1) + pltpu.roll(lo, 2 * REP, 1)).astype(BF16)


def _prompt_kernel(distance, ids_ref, q_ref, own_hbm, par_hbm, o_ref, kv_ref, s_ref, sem):
    zs, row_dev = q_ref.shape[:2]
    per = zs // 2
    rows = per * row_dev
    span = own_hbm.shape[2]
    width = 2 * HD
    n_y = own_hbm.shape[3] // width
    at = pl.multiple_of(lax.rem(lax.axis_index("y") + distance, n_y) * width, width)
    copies = []
    for which in range(2):
        for k, ref in enumerate((own_hbm, par_hbm)):
            copy = pltpu.make_async_copy(
                ref.at[:, which, :, pl.ds(at, width)],
                kv_ref.at[which, :, pl.ds(k * span, span), :],
                sem.at[2 * which + k],
            )
            copy.start()
            copies.append(copy)

    total = ids_ref.shape[1]
    shape = (per, row_dev, total)
    source = lax.broadcasted_iota(jnp.int32, shape, 0) * (2 * row_dev)
    source += lax.axis_index("core") * row_dev + lax.broadcasted_iota(jnp.int32, shape, 1)
    source = source.reshape(rows, total)
    lane = lax.broadcasted_iota(jnp.int32, (rows, total), 1)
    ids = jnp.broadcast_to(ids_ref[...].astype(F32), (rows, total))
    member = jnp.sum(jnp.where(lane == source, ids, 0.0), axis=1, keepdims=True)
    member = jnp.broadcast_to(member, (rows, HD))
    lane = lax.broadcasted_iota(jnp.int32, (rows, HD), 1)

    def scores(h):
        q = q_ref[h * per : (h + 1) * per].reshape(rows, REP * HD)
        q = jnp.concatenate([q[:, r * HD : (r + 1) * HD] for r in range(REP)], axis=0)
        one = jnp.concatenate([member] * REP, axis=0)
        q = jnp.concatenate([q * (1.0 - one).astype(BF16), q * one.astype(BF16)], axis=1)
        lanes = slice(h * HD, (h + 1) * HD)
        k = jnp.concatenate([kv_ref[0, 0, :, lanes], kv_ref[0, 1, :, lanes]], axis=1)
        s = _dot_t(q, k)
        s_ref[h] = s
        return jnp.max(s, axis=1, keepdims=True) * C2

    def attend(h, peak):
        w = jnp.exp2(s_ref[h] * C2 - peak)
        totals = jnp.sum(w, axis=1, keepdims=True)
        lanes = slice(h * HD, (h + 1) * HD)
        v = jnp.concatenate([kv_ref[1, 0, :, lanes], kv_ref[1, 1, :, lanes]], axis=1)
        acc = jnp.dot(w.astype(BF16), v, preferred_element_type=F32)
        inverse = 1.0 / totals
        weight = jnp.ones((rows, HD), F32)
        top = jnp.zeros((rows, HD), F32)
        zone = slice(h * per, (h + 1) * per)
        for r in range(REP):
            sl = slice(r * rows, (r + 1) * rows)
            o = jnp.where(member > 0.5, acc[sl, HD:], acc[sl, :HD]) * inverse[sl]
            o_ref[zone, :, r * HD : (r + 1) * HD] = o.astype(BF16).reshape(per, row_dev, HD)
            weight = jnp.where(lane == r, totals[sl], weight)
            top = jnp.where(lane == r, peak[sl], top)
        stats = _stats(top + jnp.log2(weight))
        o_ref[zone, :, REP * HD :] = stats.reshape(per, row_dev, HD)

    copies[0].wait()
    copies[1].wait()
    peak0 = scores(0)
    peak1 = scores(1)
    copies[2].wait()
    copies[3].wait()
    attend(0, peak0)
    attend(1, peak1)


def _prompt(distance, ids, q, own, par):
    zs, row_dev, width = q.shape
    span = own.shape[2]
    rows = zs // 2 * row_dev
    vmem = pl.BlockSpec(memory_space=pltpu.VMEM)
    hbm = pl.BlockSpec(memory_space=pl.ANY)
    return pl.pallas_call(
        functools.partial(_prompt_kernel, distance),
        out_shape=jax.ShapeDtypeStruct((zs, row_dev, width + HD), BF16),
        in_specs=[vmem, vmem, hbm, hbm],
        out_specs=vmem,
        scratch_shapes=[
            pltpu.VMEM((2, 2, 2 * span, 2 * HD), BF16),
            pltpu.VMEM((2, rows * REP, 2 * span), F32),
            pltpu.SemaphoreType.DMA((4,)),
        ],
        compiler_params=pltpu.CompilerParams(vmem_limit_bytes=58 * 2**20),
        cost_estimate=pl.CostEstimate(
            flops=2 * 2 * 2 * rows * REP * 2 * span * 2 * HD,
            bytes_accessed=2 * 2 * 4 * span * HD * 2,
            transcendentals=2 * rows * REP * 2 * span,
        ),
    )(ids, q, own, par)


def _lse(x):
    s = x.astype(F32)
    return s + pltpu.roll(s, HD - REP, 1) + pltpu.roll(s, HD - 2 * REP, 1)


def _weights(l2s):
    top = functools.reduce(jnp.maximum, l2s)
    es = [jnp.exp2(l2 - top) for l2 in l2s]
    total = functools.reduce(jnp.add, es)
    return [e / total for e in es], top + jnp.log2(total)


def _merge_kernel(a_ref, b_ref, c_ref, d_ref, o_ref):
    lead = a_ref.shape[:2]
    rows = lead[0] * lead[1]
    refs = (a_ref, b_ref, c_ref, d_ref)
    lane = lax.broadcasted_iota(jnp.int32, (rows, HD), 1)
    l2s = [_lse(ref[:, :, REP * HD :].reshape(rows, HD)) for ref in refs]
    l2s = [jnp.where(lane < REP, x, 0.0) for x in l2s]
    ws, l2 = _weights(l2s)
    for r in range(REP):
        acc = None
        for w, ref in zip(ws, refs):
            x = ref[:, :, r * HD : (r + 1) * HD].reshape(rows, HD).astype(F32)
            x = x * w[:, r : r + 1]
            acc = x if acc is None else acc + x
        o_ref[:, :, r * HD : (r + 1) * HD] = acc.astype(BF16).reshape(*lead, HD)
    o_ref[:, :, REP * HD :] = _stats(l2).reshape(*lead, HD)


def _merge(parts):
    return pl.pallas_call(
        _merge_kernel,
        out_shape=jax.ShapeDtypeStruct(parts[0].shape, BF16),
        compiler_params=pltpu.CompilerParams(vmem_limit_bytes=58 * 2**20),
    )(*parts)


def _final_kernel(p_ref, so_ref, sl_ref, o_ref):
    n = p_ref.shape[0]
    rows = p_ref.shape[1]
    lane = lax.broadcasted_iota(jnp.int32, (rows, HD), 1)
    l2s = [_lse(p_ref[i, :, REP * HD :]) for i in range(n)] + [sl_ref[...]]
    ws, _ = _weights([jnp.where(lane < REP, x, 0.0) for x in l2s])
    for r in range(REP):
        sl = slice(r * HD, (r + 1) * HD)
        acc = so_ref[:, sl] * ws[n][:, r : r + 1]
        for i in range(n):
            acc += p_ref[i, :, sl].astype(F32) * ws[i][:, r : r + 1]
        o_ref[:, sl] = acc.astype(BF16)


def _final(parts, suffix_o, suffix_l2):
    return pl.pallas_call(
        _final_kernel,
        out_shape=jax.ShapeDtypeStruct(suffix_o.shape, BF16),
        compiler_params=pltpu.CompilerParams(vmem_limit_bytes=58 * 2**20),
    )(parts, suffix_o, suffix_l2)


def _suffix(q, kv, lengths):
    rows, suf = kv.shape[0], kv.shape[1]
    own_q = q.reshape(rows, REP, HD)
    scores = jnp.einsum("rhd,rsd->rhs", own_q, kv[:, :, 0], preferred_element_type=F32) * C2
    valid = jnp.arange(suf, dtype=jnp.int32)[None, None, :] < lengths[:, None, None]
    scores = jnp.where(valid, scores, -BIG)
    peak = jnp.max(scores, axis=2, keepdims=True)
    probs = jnp.exp2(scores - peak)
    total = jnp.sum(probs, axis=2)
    numer = jnp.einsum("rhs,rsd->rhd", probs.astype(BF16), kv[:, :, 1], preferred_element_type=F32)
    o = (numer / total[:, :, None]).reshape(rows, REP * HD)
    l2 = jnp.pad(peak[:, :, 0] + jnp.log2(total), ((0, 0), (0, HD - REP)))
    return o, l2


def _shards(queries, prompt_kv, suffix_kv, suffix_len, group_of):
    n_y = lax.axis_size("y")
    q = queries[0]
    own = jnp.transpose(prompt_kv[0], (0, 2, 1, 3))
    par = lax.ppermute(own, "core", [(0, 1), (1, 0)])

    n_z = lax.axis_size("zh") * lax.axis_size("zl")
    spread = jnp.broadcast_to(q[None], (n_z, *q.shape))
    q0 = lax.all_to_all(spread, ("zh", "zl"), 0, 0, tiled=True)
    qs = [q0] + [
        lax.ppermute(q0, "y", [((i + d) % n_y, i) for i in range(n_y)]) for d in range(1, n_y)
    ]

    suffix_o, suffix_l2 = _suffix(q, suffix_kv[0], suffix_len[0])

    parts = []
    for d in range(n_y):
        part = _prompt(d, group_of, qs[d], own, par)
        if d:
            part = lax.ppermute(part, "y", [(i, (i + d) % n_y) for i in range(n_y)])
        parts.append(part)
    merged = _merge(parts)
    got = lax.all_to_all(merged, ("zh", "zl"), 0, 0, tiled=True)
    return _final(got, suffix_o, suffix_l2)[None]


def solution(mesh):
    fine = Mesh(
        np.asarray(mesh.devices).reshape(4, 2, 4, 2, 4), ("y", "zh", "zl", "core", "grp")
    )
    ctx, dec = ("y", "zh"), ("zl", "core")
    placed = (
        P("grp", dec, ctx),
        P("grp", None, ctx + dec, None, None),
        P("grp", dec, None, None, ctx),
        P("grp", dec),
        P("grp", None),
    )
    return jax.shard_map(
        _shards, mesh=fine, in_specs=placed, out_specs=P("grp", dec, ctx), check_vma=False
    )
```

```python
import functools
import math

import jax
import jax.numpy as jnp
import numpy as np
from jax import lax
from jax.experimental import pallas as pl
from jax.experimental.pallas import tpu as pltpu
from jax.sharding import Mesh
from jax.sharding import PartitionSpec as P

HD = 128
REP = 8
C2 = HD ** (-0.5) * math.log2(math.e)
BIG = 1e30
VMEM_LIMIT = 28 * 2**20
F32 = jnp.float32
BF16 = jnp.bfloat16


def _dot_t(a, b):
    return lax.dot_general(a, b, (((1,), (1,)), ((), ())), preferred_element_type=F32)


def _pack(l2):
    hi = l2.astype(BF16).astype(F32)
    rest = l2 - hi
    mid = rest.astype(BF16).astype(F32)
    return hi, mid, rest - mid


def _stats(l2):
    lane = lax.broadcasted_iota(jnp.int32, l2.shape, 1)
    hi, mid, lo = _pack(jnp.where(lane < REP, l2, 0.0))
    return (hi + pltpu.roll(mid, REP, 1) + pltpu.roll(lo, 2 * REP, 1)).astype(BF16)


def _prompt_kernel(distances, ids_ref, *refs):
    n = len(distances)
    q_refs, (own_hbm, par_hbm), o_refs = refs[:n], refs[n : n + 2], refs[n + 2 : 2 * n + 2]
    kv_ref, s_ref, sem = refs[2 * n + 2 :]
    zs, row_dev = q_refs[0].shape[:2]
    per = zs // 2
    rows = per * row_dev
    span = own_hbm.shape[2]
    width = 2 * HD
    n_y = own_hbm.shape[3] // width
    y = lax.axis_index("y")
    copies = []
    for i, distance in enumerate(distances):
        at = pl.multiple_of(lax.rem(y + distance, n_y) * width, width)
        for which in range(2):
            for k, ref in enumerate((own_hbm, par_hbm)):
                copy = pltpu.make_async_copy(
                    ref.at[:, which, :, pl.ds(at, width)],
                    kv_ref.at[i, which, :, pl.ds(k * span, span), :],
                    sem.at[len(copies)],
                )
                copy.start()
                copies.append(copy)

    total = ids_ref.shape[1]
    shape = (per, row_dev, total)
    source = lax.broadcasted_iota(jnp.int32, shape, 0) * (2 * row_dev)
    source += lax.axis_index("core") * row_dev + lax.broadcasted_iota(jnp.int32, shape, 1)
    source = source.reshape(rows, total)
    lane = lax.broadcasted_iota(jnp.int32, (rows, total), 1)
    ids = jnp.broadcast_to(ids_ref[...].astype(F32), (rows, total))
    member = jnp.sum(jnp.where(lane == source, ids, 0.0), axis=1, keepdims=True)
    member = jnp.broadcast_to(member, (rows, HD))
    lane = lax.broadcasted_iota(jnp.int32, (rows, HD), 1)
    keep = ((1.0 - member).astype(BF16), member.astype(BF16))

    def scores(i, h):
        q = q_refs[i][h * per : (h + 1) * per].reshape(rows, REP * HD)
        lanes = slice(h * HD, (h + 1) * HD)
        k = jnp.concatenate([kv_ref[i, 0, 0, :, lanes], kv_ref[i, 0, 1, :, lanes]], axis=1)
        tops = []
        half = REP // 2
        for part in range(2):
            block = [q[:, r * HD : (r + 1) * HD] for r in range(part * half, (part + 1) * half)]
            block = [jnp.concatenate([x * keep[0], x * keep[1]], axis=1) for x in block]
            s = _dot_t(jnp.concatenate(block, axis=0), k)
            s_ref[h, part * half * rows : (part + 1) * half * rows] = s
            tops.append(jnp.max(s, axis=1, keepdims=True) * C2)
        return jnp.concatenate(tops, axis=0)

    def attend(i, h, peak):
        w = jnp.exp2(s_ref[h] * C2 - peak)
        totals = jnp.sum(w, axis=1, keepdims=True)
        lanes = slice(h * HD, (h + 1) * HD)
        v = jnp.concatenate([kv_ref[i, 1, 0, :, lanes], kv_ref[i, 1, 1, :, lanes]], axis=1)
        acc = jnp.dot(w.astype(BF16), v, preferred_element_type=F32)
        inverse = 1.0 / totals
        weight = jnp.ones((rows, HD), F32)
        top = jnp.zeros((rows, HD), F32)
        zone = slice(h * per, (h + 1) * per)
        for r in range(REP):
            sl = slice(r * rows, (r + 1) * rows)
            o = jnp.where(member > 0.5, acc[sl, HD:], acc[sl, :HD]) * inverse[sl]
            o = o.astype(BF16).reshape(per, row_dev, HD)
            o_refs[i][zone, :, r * HD : (r + 1) * HD] = o
            weight = jnp.where(lane == r, totals[sl], weight)
            top = jnp.where(lane == r, peak[sl], top)
        stats = _stats(top + jnp.log2(weight))
        o_refs[i][zone, :, REP * HD :] = stats.reshape(per, row_dev, HD)

    for i in range(n):
        for copy in copies[4 * i : 4 * i + 4]:
            copy.wait()
        peaks = [scores(i, h) for h in range(2)]
        for h in range(2):
            attend(i, h, peaks[h])


def _prompt(distances, ids, qs, own, par):
    n = len(distances)
    zs, row_dev, width = qs[0].shape
    span = own.shape[2]
    rows = zs // 2 * row_dev
    vmem = pl.BlockSpec(memory_space=pltpu.VMEM)
    hbm = pl.BlockSpec(memory_space=pl.ANY)
    return pl.pallas_call(
        functools.partial(_prompt_kernel, distances),
        out_shape=[jax.ShapeDtypeStruct((zs, row_dev, width + HD), BF16)] * n,
        in_specs=[vmem] * (n + 1) + [hbm, hbm],
        out_specs=[vmem] * n,
        scratch_shapes=[
            pltpu.VMEM((n, 2, 2, 2 * span, 2 * HD), BF16),
            pltpu.VMEM((2, rows * REP, 2 * span), F32),
            pltpu.SemaphoreType.DMA((4 * n,)),
        ],
        compiler_params=pltpu.CompilerParams(vmem_limit_bytes=VMEM_LIMIT),
        cost_estimate=pl.CostEstimate(
            flops=n * 2 * 2 * 2 * rows * REP * 2 * span * 2 * HD,
            bytes_accessed=n * 2 * 2 * 4 * span * HD * 2,
            transcendentals=n * 2 * rows * REP * 2 * span,
        ),
    )(ids, *qs, own, par)


def _lse(x):
    s = x.astype(F32)
    return s + pltpu.roll(s, HD - REP, 1) + pltpu.roll(s, HD - 2 * REP, 1)


def _weights(l2s):
    top = functools.reduce(jnp.maximum, l2s)
    es = [jnp.exp2(l2 - top) for l2 in l2s]
    total = functools.reduce(jnp.add, es)
    return [e / total for e in es], top + jnp.log2(total)


def _merge_kernel(a_ref, b_ref, c_ref, d_ref, o_ref):
    lead = a_ref.shape[:2]
    rows = lead[0] * lead[1]
    refs = (a_ref, b_ref, c_ref, d_ref)
    lane = lax.broadcasted_iota(jnp.int32, (rows, HD), 1)
    l2s = [_lse(ref[:, :, REP * HD :].reshape(rows, HD)) for ref in refs]
    l2s = [jnp.where(lane < REP, x, 0.0) for x in l2s]
    ws, l2 = _weights(l2s)
    for r in range(REP):
        acc = None
        for w, ref in zip(ws, refs):
            x = ref[:, :, r * HD : (r + 1) * HD].reshape(rows, HD).astype(F32)
            x = x * w[:, r : r + 1]
            acc = x if acc is None else acc + x
        o_ref[:, :, r * HD : (r + 1) * HD] = acc.astype(BF16).reshape(*lead, HD)
    o_ref[:, :, REP * HD :] = _stats(l2).reshape(*lead, HD)


def _merge(parts):
    return pl.pallas_call(
        _merge_kernel,
        out_shape=jax.ShapeDtypeStruct(parts[0].shape, BF16),
        compiler_params=pltpu.CompilerParams(vmem_limit_bytes=VMEM_LIMIT),
    )(*parts)


def _final_kernel(p_ref, so_ref, sl_ref, o_ref):
    n = p_ref.shape[0]
    rows = p_ref.shape[1]
    lane = lax.broadcasted_iota(jnp.int32, (rows, HD), 1)
    l2s = [_lse(p_ref[i, :, REP * HD :]) for i in range(n)] + [sl_ref[...]]
    ws, _ = _weights([jnp.where(lane < REP, x, 0.0) for x in l2s])
    for r in range(REP):
        sl = slice(r * HD, (r + 1) * HD)
        acc = so_ref[:, sl] * ws[n][:, r : r + 1]
        for i in range(n):
            acc += p_ref[i, :, sl].astype(F32) * ws[i][:, r : r + 1]
        o_ref[:, sl] = acc.astype(BF16)


def _final(parts, suffix_o, suffix_l2):
    return pl.pallas_call(
        _final_kernel,
        out_shape=jax.ShapeDtypeStruct(suffix_o.shape, BF16),
        compiler_params=pltpu.CompilerParams(vmem_limit_bytes=VMEM_LIMIT),
    )(parts, suffix_o, suffix_l2)


def _suffix(q, kv, lengths):
    rows, suf = kv.shape[0], kv.shape[1]
    own_q = q.reshape(rows, REP, HD)
    scores = jnp.einsum("rhd,rsd->rhs", own_q, kv[:, :, 0], preferred_element_type=F32) * C2
    valid = jnp.arange(suf, dtype=jnp.int32)[None, None, :] < lengths[:, None, None]
    scores = jnp.where(valid, scores, -BIG)
    peak = jnp.max(scores, axis=2, keepdims=True)
    probs = jnp.exp2(scores - peak)
    total = jnp.sum(probs, axis=2)
    numer = jnp.einsum("rhs,rsd->rhd", probs.astype(BF16), kv[:, :, 1], preferred_element_type=F32)
    o = (numer / total[:, :, None]).reshape(rows, REP * HD)
    l2 = jnp.pad(peak[:, :, 0] + jnp.log2(total), ((0, 0), (0, HD - REP)))
    return o, l2


def _shards(queries, prompt_kv, suffix_kv, suffix_len, group_of):
    n_y = lax.axis_size("y")
    q = queries[0]
    own = jnp.transpose(prompt_kv[0], (0, 2, 1, 3))
    par = lax.ppermute(own, "core", [(0, 1), (1, 0)])

    n_z = lax.axis_size("zh") * lax.axis_size("zl")
    spread = jnp.broadcast_to(q[None], (n_z, *q.shape))
    q0 = lax.all_to_all(spread, ("zh", "zl"), 0, 0, tiled=True)
    qs = [q0] + [
        lax.ppermute(q0, "y", [((i + d) % n_y, i) for i in range(n_y)]) for d in range(1, n_y)
    ]

    suffix_o, suffix_l2 = _suffix(q, suffix_kv[0], suffix_len[0])

    away = tuple(range(1, n_y))
    parts = list(_prompt((0,), group_of, qs[:1], own, par))
    for d, part in zip(away, _prompt(away, group_of, qs[1:], own, par)):
        parts.append(lax.ppermute(part, "y", [(i, (i + d) % n_y) for i in range(n_y)]))
    merged = _merge(parts)
    got = lax.all_to_all(merged, ("zh", "zl"), 0, 0, tiled=True)
    return _final(got, suffix_o, suffix_l2)[None]


def solution(mesh):
    fine = Mesh(
        np.asarray(mesh.devices).reshape(4, 2, 4, 2, 4), ("y", "zh", "zl", "core", "grp")
    )
    ctx, dec = ("y", "zh"), ("zl", "core")
    placed = (
        P("grp", dec, ctx),
        P("grp", None, ctx + dec, None, None),
        P("grp", dec, None, None, ctx),
        P("grp", dec),
        P("grp", None),
    )
    return jax.shard_map(
        _shards, mesh=fine, in_specs=placed, out_specs=P("grp", dec, ctx), check_vma=False
    )
```

```python
import functools
import math

import jax
import jax.numpy as jnp
import numpy as np
from jax import lax
from jax.experimental import pallas as pl
from jax.experimental.pallas import tpu as pltpu
from jax.sharding import Mesh
from jax.sharding import PartitionSpec as P

HD = 128
REP = 8
C2 = HD ** (-0.5) * math.log2(math.e)
BIG = 1e30
VMEM_LIMIT = 28 * 2**20
F32 = jnp.float32
BF16 = jnp.bfloat16


def _dot_t(a, b):
    return lax.dot_general(a, b, (((1,), (1,)), ((), ())), preferred_element_type=F32)


def _pack(l2):
    hi = l2.astype(BF16).astype(F32)
    rest = l2 - hi
    mid = rest.astype(BF16).astype(F32)
    return hi, mid, rest - mid


def _stats(l2):
    lane = lax.broadcasted_iota(jnp.int32, l2.shape, 1)
    hi, mid, lo = _pack(jnp.where(lane < REP, l2, 0.0))
    return (hi + pltpu.roll(mid, REP, 1) + pltpu.roll(lo, 2 * REP, 1)).astype(BF16)


def _partners(y, core):
    a, b = y + 1 - 2 * lax.rem(y, 2), 3 - y
    return y, jnp.where(core == 0, a, b), jnp.where(core == 0, b, a), lax.rem(y + 2, 4)


def _prompt_kernel(wanted, ids_ref, *refs):
    n = len(wanted)
    q_refs, (own_hbm, par_hbm), o_refs = refs[:n], refs[n : n + 2], refs[n + 2 : 2 * n + 2]
    kv_ref, s_ref, sem = refs[2 * n + 2 :]
    zs, row_dev = q_refs[0].shape[:2]
    per = zs // 2
    rows = per * row_dev
    span = own_hbm.shape[2]
    width = 2 * HD
    core = lax.axis_index("core")
    partners = _partners(lax.axis_index("y"), core)
    copies = []
    for i, partner in enumerate(wanted):
        at = pl.multiple_of(partners[partner] * width, width)
        for which in range(2):
            for k, ref in enumerate((own_hbm, par_hbm)):
                copy = pltpu.make_async_copy(
                    ref.at[:, which, :, pl.ds(at, width)],
                    kv_ref.at[i, which, :, pl.ds(k * span, span), :],
                    sem.at[len(copies)],
                )
                copy.start()
                copies.append(copy)

    total = ids_ref.shape[1]
    shape = (per, row_dev, total)
    source = lax.broadcasted_iota(jnp.int32, shape, 0) * (2 * row_dev)
    source += core * row_dev + lax.broadcasted_iota(jnp.int32, shape, 1)
    source = source.reshape(rows, total)
    lane = lax.broadcasted_iota(jnp.int32, (rows, total), 1)
    ids = jnp.broadcast_to(ids_ref[...].astype(F32), (rows, total))
    member = jnp.sum(jnp.where(lane == source, ids, 0.0), axis=1, keepdims=True)
    member = jnp.broadcast_to(member, (rows, HD))
    lane = lax.broadcasted_iota(jnp.int32, (rows, HD), 1)
    keep = ((1.0 - member).astype(BF16), member.astype(BF16))

    def scores(i, h):
        q = q_refs[i][h * per : (h + 1) * per].reshape(rows, REP * HD)
        lanes = slice(h * HD, (h + 1) * HD)
        k = jnp.concatenate([kv_ref[i, 0, 0, :, lanes], kv_ref[i, 0, 1, :, lanes]], axis=1)
        tops = []
        half = REP // 2
        for part in range(2):
            block = [q[:, r * HD : (r + 1) * HD] for r in range(part * half, (part + 1) * half)]
            block = [jnp.concatenate([x * keep[0], x * keep[1]], axis=1) for x in block]
            s = _dot_t(jnp.concatenate(block, axis=0), k)
            s_ref[h, part * half * rows : (part + 1) * half * rows] = s
            tops.append(jnp.max(s, axis=1, keepdims=True) * C2)
        return jnp.concatenate(tops, axis=0)

    def attend(i, h, peak):
        w = jnp.exp2(s_ref[h] * C2 - peak)
        totals = jnp.sum(w, axis=1, keepdims=True)
        lanes = slice(h * HD, (h + 1) * HD)
        v = jnp.concatenate([kv_ref[i, 1, 0, :, lanes], kv_ref[i, 1, 1, :, lanes]], axis=1)
        acc = jnp.dot(w.astype(BF16), v, preferred_element_type=F32)
        inverse = 1.0 / totals
        weight = jnp.ones((rows, HD), F32)
        top = jnp.zeros((rows, HD), F32)
        zone = slice(h * per, (h + 1) * per)
        for r in range(REP):
            sl = slice(r * rows, (r + 1) * rows)
            o = jnp.where(member > 0.5, acc[sl, HD:], acc[sl, :HD]) * inverse[sl]
            o = o.astype(BF16).reshape(per, row_dev, HD)
            o_refs[i][zone, :, r * HD : (r + 1) * HD] = o
            weight = jnp.where(lane == r, totals[sl], weight)
            top = jnp.where(lane == r, peak[sl], top)
        stats = _stats(top + jnp.log2(weight))
        o_refs[i][zone, :, REP * HD :] = stats.reshape(per, row_dev, HD)

    for i in range(n):
        for copy in copies[4 * i : 4 * i + 4]:
            copy.wait()
        peaks = [scores(i, h) for h in range(2)]
        for h in range(2):
            attend(i, h, peaks[h])


def _prompt(wanted, ids, qs, own, par):
    n = len(wanted)
    zs, row_dev, width = qs[0].shape
    span = own.shape[2]
    rows = zs // 2 * row_dev
    vmem = pl.BlockSpec(memory_space=pltpu.VMEM)
    hbm = pl.BlockSpec(memory_space=pl.ANY)
    return pl.pallas_call(
        functools.partial(_prompt_kernel, wanted),
        out_shape=[jax.ShapeDtypeStruct((zs, row_dev, width + HD), BF16)] * n,
        in_specs=[vmem] * (n + 1) + [hbm, hbm],
        out_specs=[vmem] * n,
        scratch_shapes=[
            pltpu.VMEM((n, 2, 2, 2 * span, 2 * HD), BF16),
            pltpu.VMEM((2, rows * REP, 2 * span), F32),
            pltpu.SemaphoreType.DMA((4 * n,)),
        ],
        compiler_params=pltpu.CompilerParams(vmem_limit_bytes=VMEM_LIMIT),
        cost_estimate=pl.CostEstimate(
            flops=n * 2 * 2 * 2 * rows * REP * 2 * span * 2 * HD,
            bytes_accessed=n * 2 * 2 * 4 * span * HD * 2,
            transcendentals=n * 2 * rows * REP * 2 * span,
        ),
    )(ids, *qs, own, par)


def _lse(x):
    s = x.astype(F32)
    return s + pltpu.roll(s, HD - REP, 1) + pltpu.roll(s, HD - 2 * REP, 1)


def _weights(l2s):
    top = functools.reduce(jnp.maximum, l2s)
    es = [jnp.exp2(l2 - top) for l2 in l2s]
    total = functools.reduce(jnp.add, es)
    return [e / total for e in es], top + jnp.log2(total)


def _merge_kernel(*all_refs):
    *refs, o_ref = all_refs
    lead = o_ref.shape[:2]
    rows = lead[0] * lead[1]
    lane = lax.broadcasted_iota(jnp.int32, (rows, HD), 1)
    l2s = [_lse(ref[:, :, REP * HD :].reshape(rows, HD)) for ref in refs]
    l2s = [jnp.where(lane < REP, x, 0.0) for x in l2s]
    ws, l2 = _weights(l2s)
    for r in range(REP):
        acc = None
        for w, ref in zip(ws, refs):
            x = ref[:, :, r * HD : (r + 1) * HD].reshape(rows, HD).astype(F32)
            x = x * w[:, r : r + 1]
            acc = x if acc is None else acc + x
        o_ref[:, :, r * HD : (r + 1) * HD] = acc.astype(BF16).reshape(*lead, HD)
    o_ref[:, :, REP * HD :] = _stats(l2).reshape(*lead, HD)


def _merge(parts):
    return pl.pallas_call(
        _merge_kernel,
        out_shape=jax.ShapeDtypeStruct(parts[0].shape, BF16),
        compiler_params=pltpu.CompilerParams(vmem_limit_bytes=VMEM_LIMIT),
    )(*parts)


def _final_kernel(p_ref, so_ref, sl_ref, o_ref):
    n = p_ref.shape[0]
    rows = p_ref.shape[1]
    lane = lax.broadcasted_iota(jnp.int32, (rows, HD), 1)
    l2s = [_lse(p_ref[i, :, REP * HD :]) for i in range(n)] + [sl_ref[...]]
    ws, _ = _weights([jnp.where(lane < REP, x, 0.0) for x in l2s])
    for r in range(REP):
        sl = slice(r * HD, (r + 1) * HD)
        acc = so_ref[:, sl] * ws[n][:, r : r + 1]
        for i in range(n):
            acc += p_ref[i, :, sl].astype(F32) * ws[i][:, r : r + 1]
        o_ref[:, sl] = acc.astype(BF16)


def _final(parts, suffix_o, suffix_l2):
    return pl.pallas_call(
        _final_kernel,
        out_shape=jax.ShapeDtypeStruct(suffix_o.shape, BF16),
        compiler_params=pltpu.CompilerParams(vmem_limit_bytes=VMEM_LIMIT),
    )(parts, suffix_o, suffix_l2)


def _suffix(q, kv, lengths):
    rows, suf = kv.shape[0], kv.shape[1]
    own_q = q.reshape(rows, REP, HD)
    scores = jnp.einsum("rhd,rsd->rhs", own_q, kv[:, :, 0], preferred_element_type=F32) * C2
    valid = jnp.arange(suf, dtype=jnp.int32)[None, None, :] < lengths[:, None, None]
    scores = jnp.where(valid, scores, -BIG)
    peak = jnp.max(scores, axis=2, keepdims=True)
    probs = jnp.exp2(scores - peak)
    total = jnp.sum(probs, axis=2)
    numer = jnp.einsum("rhs,rsd->rhd", probs.astype(BF16), kv[:, :, 1], preferred_element_type=F32)
    o = (numer / total[:, :, None]).reshape(rows, REP * HD)
    l2 = jnp.pad(peak[:, :, 0] + jnp.log2(total), ((0, 0), (0, HD - REP)))
    return o, l2


def _pairs(which):
    out = []
    for y in range(4):
        for core in range(2):
            to = 3 - y if (which == 1) == (core == 1) else y ^ 1
            out.append((2 * y + core, 2 * to + core))
    return out


def _shards(queries, prompt_kv, suffix_kv, suffix_len, group_of):
    q = queries[0]
    own = jnp.transpose(prompt_kv[0], (0, 2, 1, 3))

    n_z = lax.axis_size("zh") * lax.axis_size("zl")
    spread = jnp.broadcast_to(q[None], (n_z, *q.shape))
    q0 = lax.all_to_all(spread, ("zh", "zl"), 0, 0, tiled=True)
    q0, own = lax.optimization_barrier((q0, own))
    par = lax.ppermute(own, "core", [(0, 1), (1, 0)])
    first = lax.ppermute(q0, ("y", "core"), _pairs(1))
    second = lax.ppermute(q0, ("y", "core"), _pairs(2))
    third = lax.ppermute(first, ("y", "core"), _pairs(2))

    suffix_o, suffix_l2 = _suffix(q, suffix_kv[0], suffix_len[0])

    def part(which, block):
        return _prompt((which,), group_of, [block], own, par)[0]

    part_second, third = lax.optimization_barrier((part(2, second), third))
    back_second = lax.ppermute(part_second, ("y", "core"), _pairs(2))
    back_third = lax.ppermute(part(3, third), ("y", "core"), _pairs(2))
    merged = _merge([part(1, first), back_third])
    back_first = lax.ppermute(merged, ("y", "core"), _pairs(1))
    merged = _merge([part(0, q0), back_second, back_first])
    got = lax.all_to_all(merged, ("zh", "zl"), 0, 0, tiled=True)
    return _final(got, suffix_o, suffix_l2)[None]


def solution(mesh):
    fine = Mesh(
        np.asarray(mesh.devices).reshape(4, 2, 4, 2, 4), ("y", "zh", "zl", "core", "grp")
    )
    ctx, dec = ("y", "zh"), ("zl", "core")
    placed = (
        P("grp", dec, ctx),
        P("grp", None, ctx + dec, None, None),
        P("grp", dec, None, None, ctx),
        P("grp", dec),
        P("grp", None),
    )
    return jax.shard_map(
        _shards, mesh=fine, in_specs=placed, out_specs=P("grp", dec, ctx), check_vma=False
    )
```

```python
import functools
import math

import jax
import jax.numpy as jnp
import numpy as np
from jax import lax
from jax.experimental import pallas as pl
from jax.experimental.pallas import tpu as pltpu
from jax.sharding import Mesh
from jax.sharding import PartitionSpec as P

HD = 128
REP = 8
C2 = HD ** (-0.5) * math.log2(math.e)
BIG = 1e30
VMEM_LIMIT = 28 * 2**20
F32 = jnp.float32
BF16 = jnp.bfloat16


def _dot_t(a, b):
    return lax.dot_general(a, b, (((1,), (1,)), ((), ())), preferred_element_type=F32)


def _pack(l2):
    hi = l2.astype(BF16).astype(F32)
    rest = l2 - hi
    mid = rest.astype(BF16).astype(F32)
    return hi, mid, rest - mid


def _stats(l2):
    lane = lax.broadcasted_iota(jnp.int32, l2.shape, 1)
    hi, mid, lo = _pack(jnp.where(lane < REP, l2, 0.0))
    return (hi + pltpu.roll(mid, REP, 1) + pltpu.roll(lo, 2 * REP, 1)).astype(BF16)


def _partners(y, core):
    a, b = y + 1 - 2 * lax.rem(y, 2), 3 - y
    return y, jnp.where(core == 0, a, b), jnp.where(core == 0, b, a), lax.rem(y + 2, 4)


def _prompt_kernel(wanted, ids_ref, *refs):
    n = len(wanted)
    q_refs, (own_hbm, par_hbm), o_refs = refs[:n], refs[n : n + 2], refs[n + 2 : 2 * n + 2]
    kv_ref, s_ref, sem = refs[2 * n + 2 :]
    zs, row_dev = q_refs[0].shape[:2]
    per = zs // 2
    rows = per * row_dev
    span = own_hbm.shape[2]
    width = 2 * HD
    core = lax.axis_index("core")
    partners = _partners(lax.axis_index("y"), core)
    copies = []
    for i, partner in enumerate(wanted):
        at = pl.multiple_of(partners[partner] * width, width)
        for which in range(2):
            for k, ref in enumerate((own_hbm, par_hbm)):
                copy = pltpu.make_async_copy(
                    ref.at[:, which, :, pl.ds(at, width)],
                    kv_ref.at[i, which, :, pl.ds(k * span, span), :],
                    sem.at[len(copies)],
                )
                copy.start()
                copies.append(copy)

    total = ids_ref.shape[1]
    shape = (per, row_dev, total)
    source = lax.broadcasted_iota(jnp.int32, shape, 0) * (2 * row_dev)
    source += core * row_dev + lax.broadcasted_iota(jnp.int32, shape, 1)
    source = source.reshape(rows, total)
    lane = lax.broadcasted_iota(jnp.int32, (rows, total), 1)
    ids = jnp.broadcast_to(ids_ref[...].astype(F32), (rows, total))
    member = jnp.sum(jnp.where(lane == source, ids, 0.0), axis=1, keepdims=True)
    member = jnp.broadcast_to(member, (rows, HD))
    lane = lax.broadcasted_iota(jnp.int32, (rows, HD), 1)
    keep = ((1.0 - member).astype(BF16), member.astype(BF16))

    def scores(i, h):
        q = q_refs[i][h * per : (h + 1) * per].reshape(rows, REP * HD)
        lanes = slice(h * HD, (h + 1) * HD)
        k = jnp.concatenate([kv_ref[i, 0, 0, :, lanes], kv_ref[i, 0, 1, :, lanes]], axis=1)
        tops = []
        half = REP // 2
        for part in range(2):
            block = [q[:, r * HD : (r + 1) * HD] for r in range(part * half, (part + 1) * half)]
            block = [jnp.concatenate([x * keep[0], x * keep[1]], axis=1) for x in block]
            s = _dot_t(jnp.concatenate(block, axis=0), k)
            s_ref[h, part * half * rows : (part + 1) * half * rows] = s
            tops.append(jnp.max(s, axis=1, keepdims=True) * C2)
        return jnp.concatenate(tops, axis=0)

    def attend(i, h, peak):
        w = jnp.exp2(s_ref[h] * C2 - peak)
        totals = jnp.sum(w, axis=1, keepdims=True)
        lanes = slice(h * HD, (h + 1) * HD)
        v = jnp.concatenate([kv_ref[i, 1, 0, :, lanes], kv_ref[i, 1, 1, :, lanes]], axis=1)
        acc = jnp.dot(w.astype(BF16), v, preferred_element_type=F32)
        inverse = 1.0 / totals
        weight = jnp.ones((rows, HD), F32)
        top = jnp.zeros((rows, HD), F32)
        zone = slice(h * per, (h + 1) * per)
        for r in range(REP):
            sl = slice(r * rows, (r + 1) * rows)
            o = jnp.where(member > 0.5, acc[sl, HD:], acc[sl, :HD]) * inverse[sl]
            o = o.astype(BF16).reshape(per, row_dev, HD)
            o_refs[i][zone, :, r * HD : (r + 1) * HD] = o
            weight = jnp.where(lane == r, totals[sl], weight)
            top = jnp.where(lane == r, peak[sl], top)
        stats = _stats(top + jnp.log2(weight))
        o_refs[i][zone, :, REP * HD :] = stats.reshape(per, row_dev, HD)

    for i in range(n):
        for copy in copies[4 * i : 4 * i + 4]:
            copy.wait()
        peaks = [scores(i, h) for h in range(2)]
        for h in range(2):
            attend(i, h, peaks[h])


def _prompt(wanted, ids, qs, own, par):
    n = len(wanted)
    zs, row_dev, width = qs[0].shape
    span = own.shape[2]
    rows = zs // 2 * row_dev
    vmem = pl.BlockSpec(memory_space=pltpu.VMEM)
    hbm = pl.BlockSpec(memory_space=pl.ANY)
    return pl.pallas_call(
        functools.partial(_prompt_kernel, wanted),
        out_shape=[jax.ShapeDtypeStruct((zs, row_dev, width + HD), BF16)] * n,
        in_specs=[vmem] * (n + 1) + [hbm, hbm],
        out_specs=[vmem] * n,
        scratch_shapes=[
            pltpu.VMEM((n, 2, 2, 2 * span, 2 * HD), BF16),
            pltpu.VMEM((2, rows * REP, 2 * span), F32),
            pltpu.SemaphoreType.DMA((4 * n,)),
        ],
        compiler_params=pltpu.CompilerParams(vmem_limit_bytes=VMEM_LIMIT),
        cost_estimate=pl.CostEstimate(
            flops=n * 2 * 2 * 2 * rows * REP * 2 * span * 2 * HD,
            bytes_accessed=n * 2 * 2 * 4 * span * HD * 2,
            transcendentals=n * 2 * rows * REP * 2 * span,
        ),
    )(ids, *qs, own, par)


def _lse(x):
    s = x.astype(F32)
    return s + pltpu.roll(s, HD - REP, 1) + pltpu.roll(s, HD - 2 * REP, 1)


def _weights(l2s):
    top = functools.reduce(jnp.maximum, l2s)
    es = [jnp.exp2(l2 - top) for l2 in l2s]
    total = functools.reduce(jnp.add, es)
    return [e / total for e in es], top + jnp.log2(total)


def _merge_kernel(*all_refs):
    *refs, o_ref = all_refs
    lead = o_ref.shape[:2]
    rows = lead[0] * lead[1]
    lane = lax.broadcasted_iota(jnp.int32, (rows, HD), 1)
    l2s = [_lse(ref[:, :, REP * HD :].reshape(rows, HD)) for ref in refs]
    l2s = [jnp.where(lane < REP, x, 0.0) for x in l2s]
    ws, l2 = _weights(l2s)
    for r in range(REP):
        acc = None
        for w, ref in zip(ws, refs):
            x = ref[:, :, r * HD : (r + 1) * HD].reshape(rows, HD).astype(F32)
            x = x * w[:, r : r + 1]
            acc = x if acc is None else acc + x
        o_ref[:, :, r * HD : (r + 1) * HD] = acc.astype(BF16).reshape(*lead, HD)
    o_ref[:, :, REP * HD :] = _stats(l2).reshape(*lead, HD)


def _merge(parts):
    return pl.pallas_call(
        _merge_kernel,
        out_shape=jax.ShapeDtypeStruct(parts[0].shape, BF16),
        compiler_params=pltpu.CompilerParams(vmem_limit_bytes=VMEM_LIMIT),
    )(*parts)


def _final_kernel(p_ref, so_ref, sl_ref, o_ref):
    n = p_ref.shape[0]
    rows = p_ref.shape[1]
    lane = lax.broadcasted_iota(jnp.int32, (rows, HD), 1)
    l2s = [_lse(p_ref[i, :, REP * HD :]) for i in range(n)] + [sl_ref[...]]
    ws, _ = _weights([jnp.where(lane < REP, x, 0.0) for x in l2s])
    for r in range(REP):
        sl = slice(r * HD, (r + 1) * HD)
        acc = so_ref[:, sl] * ws[n][:, r : r + 1]
        for i in range(n):
            acc += p_ref[i, :, sl].astype(F32) * ws[i][:, r : r + 1]
        o_ref[:, sl] = acc.astype(BF16)


def _final(parts, suffix_o, suffix_l2):
    return pl.pallas_call(
        _final_kernel,
        out_shape=jax.ShapeDtypeStruct(suffix_o.shape, BF16),
        compiler_params=pltpu.CompilerParams(vmem_limit_bytes=VMEM_LIMIT),
    )(parts, suffix_o, suffix_l2)


def _suffix(q, kv, lengths):
    rows, suf = kv.shape[0], kv.shape[1]
    own_q = q.reshape(rows, REP, HD)
    scores = jnp.einsum("rhd,rsd->rhs", own_q, kv[:, :, 0], preferred_element_type=F32) * C2
    valid = jnp.arange(suf, dtype=jnp.int32)[None, None, :] < lengths[:, None, None]
    scores = jnp.where(valid, scores, -BIG)
    peak = jnp.max(scores, axis=2, keepdims=True)
    probs = jnp.exp2(scores - peak)
    total = jnp.sum(probs, axis=2)
    numer = jnp.einsum("rhs,rsd->rhd", probs.astype(BF16), kv[:, :, 1], preferred_element_type=F32)
    o = (numer / total[:, :, None]).reshape(rows, REP * HD)
    l2 = jnp.pad(peak[:, :, 0] + jnp.log2(total), ((0, 0), (0, HD - REP)))
    return o, l2


def _pairs(which):
    out = []
    for y in range(4):
        for core in range(2):
            to = 3 - y if (which == 1) == (core == 1) else y ^ 1
            out.append((2 * y + core, 2 * to + core))
    return out


def _shards(queries, prompt_kv, suffix_kv, suffix_len, group_of):
    q = queries[0]
    own = jnp.transpose(prompt_kv[0], (0, 2, 1, 3))

    n_z = lax.axis_size("zh") * lax.axis_size("zl")
    spread = jnp.broadcast_to(q[None], (n_z, *q.shape))
    q0 = lax.all_to_all(spread, ("zh", "zl"), 0, 0, tiled=True)
    q0, own = lax.optimization_barrier((q0, own))
    par = lax.ppermute(own, "core", [(0, 1), (1, 0)])
    first = lax.ppermute(q0, ("y", "core"), _pairs(1))
    second = lax.ppermute(q0, ("y", "core"), _pairs(2))
    third = lax.ppermute(first, ("y", "core"), _pairs(2))

    def part(which, block):
        return _prompt((which,), group_of, [block], own, par)[0]

    part_second, third = lax.optimization_barrier((part(2, second), third))
    back_second = lax.ppermute(part_second, ("y", "core"), _pairs(2))
    back_third = lax.ppermute(part(3, third), ("y", "core"), _pairs(2))
    merged = _merge([part(1, first), back_third])
    back_first = lax.ppermute(merged, ("y", "core"), _pairs(1))
    merged = _merge([part(0, q0), back_second, back_first])
    merged, q, suffix_kv, suffix_len = lax.optimization_barrier(
        (merged, q, suffix_kv, suffix_len)
    )
    suffix_o, suffix_l2 = _suffix(q, suffix_kv[0], suffix_len[0])
    got = lax.all_to_all(merged, ("zh", "zl"), 0, 0, tiled=True)
    return _final(got, suffix_o, suffix_l2)[None]


def solution(mesh):
    fine = Mesh(
        np.asarray(mesh.devices).reshape(4, 2, 4, 2, 4), ("y", "zh", "zl", "core", "grp")
    )
    ctx, dec = ("y", "zh"), ("zl", "core")
    placed = (
        P("grp", dec, ctx),
        P("grp", None, ctx + dec, None, None),
        P("grp", dec, None, None, ctx),
        P("grp", dec),
        P("grp", None),
    )
    return jax.shard_map(
        _shards, mesh=fine, in_specs=placed, out_specs=P("grp", dec, ctx), check_vma=False
    )
```

```python
import functools
import math

import jax
import jax.numpy as jnp
import numpy as np
from jax import lax
from jax.experimental import pallas as pl
from jax.experimental.pallas import tpu as pltpu
from jax.sharding import Mesh
from jax.sharding import PartitionSpec as P

HD = 128
REP = 8
C2 = HD ** (-0.5) * math.log2(math.e)
BIG = 1e30
VMEM_LIMIT = 28 * 2**20
F32 = jnp.float32
BF16 = jnp.bfloat16


def _dot_t(a, b):
    return lax.dot_general(a, b, (((1,), (1,)), ((), ())), preferred_element_type=F32)


def _pack(l2):
    hi = l2.astype(BF16).astype(F32)
    rest = l2 - hi
    mid = rest.astype(BF16).astype(F32)
    return hi, mid, rest - mid


def _stats(l2):
    lane = lax.broadcasted_iota(jnp.int32, l2.shape, 1)
    hi, mid, lo = _pack(jnp.where(lane < REP, l2, 0.0))
    return (hi + pltpu.roll(mid, REP, 1) + pltpu.roll(lo, 2 * REP, 1)).astype(BF16)


def _partners(y, core):
    a, b = y + 1 - 2 * lax.rem(y, 2), 3 - y
    return y, jnp.where(core == 0, a, b), jnp.where(core == 0, b, a), lax.rem(y + 2, 4)


def _prompt_kernel(wanted, ids_ref, *refs):
    n = len(wanted)
    q_refs, (own_hbm, par_hbm), o_refs = refs[:n], refs[n : n + 2], refs[n + 2 : 2 * n + 2]
    kv_ref, s_ref, sem = refs[2 * n + 2 :]
    zs, row_dev = q_refs[0].shape[:2]
    per = zs // 2
    rows = per * row_dev
    span = own_hbm.shape[2]
    width = 2 * HD
    core = lax.axis_index("core")
    partners = _partners(lax.axis_index("y"), core)
    copies = []
    for i, partner in enumerate(wanted):
        at = pl.multiple_of(partners[partner] * width, width)
        for which in range(2):
            for k, ref in enumerate((own_hbm, par_hbm)):
                copy = pltpu.make_async_copy(
                    ref.at[:, which, :, pl.ds(at, width)],
                    kv_ref.at[i, which, :, pl.ds(k * span, span), :],
                    sem.at[len(copies)],
                )
                copy.start()
                copies.append(copy)

    total = ids_ref.shape[1]
    shape = (per, row_dev, total)
    source = lax.broadcasted_iota(jnp.int32, shape, 0) * (2 * row_dev)
    source += core * row_dev + lax.broadcasted_iota(jnp.int32, shape, 1)
    source = source.reshape(rows, total)
    lane = lax.broadcasted_iota(jnp.int32, (rows, total), 1)
    ids = jnp.broadcast_to(ids_ref[...].astype(F32), (rows, total))
    member = jnp.sum(jnp.where(lane == source, ids, 0.0), axis=1, keepdims=True)
    member = jnp.broadcast_to(member, (rows, HD))
    lane = lax.broadcasted_iota(jnp.int32, (rows, HD), 1)
    keep = ((1.0 - member).astype(BF16), member.astype(BF16))

    def scores(i, h):
        q = q_refs[i][h * per : (h + 1) * per].reshape(rows, REP * HD)
        lanes = slice(h * HD, (h + 1) * HD)
        k = jnp.concatenate([kv_ref[i, 0, 0, :, lanes], kv_ref[i, 0, 1, :, lanes]], axis=1)
        tops = []
        half = REP // 2
        for part in range(2):
            block = [q[:, r * HD : (r + 1) * HD] for r in range(part * half, (part + 1) * half)]
            block = [jnp.concatenate([x * keep[0], x * keep[1]], axis=1) for x in block]
            s = _dot_t(jnp.concatenate(block, axis=0), k)
            s_ref[h, part * half * rows : (part + 1) * half * rows] = s
            tops.append(jnp.max(s, axis=1, keepdims=True) * C2)
        return jnp.concatenate(tops, axis=0)

    def attend(i, h, peak):
        w = jnp.exp2(s_ref[h] * C2 - peak)
        totals = jnp.sum(w, axis=1, keepdims=True)
        lanes = slice(h * HD, (h + 1) * HD)
        v = jnp.concatenate([kv_ref[i, 1, 0, :, lanes], kv_ref[i, 1, 1, :, lanes]], axis=1)
        acc = jnp.dot(w.astype(BF16), v, preferred_element_type=F32)
        inverse = 1.0 / totals
        weight = jnp.ones((rows, HD), F32)
        top = jnp.zeros((rows, HD), F32)
        zone = slice(h * per, (h + 1) * per)
        for r in range(REP):
            sl = slice(r * rows, (r + 1) * rows)
            o = jnp.where(member > 0.5, acc[sl, HD:], acc[sl, :HD]) * inverse[sl]
            o = o.astype(BF16).reshape(per, row_dev, HD)
            o_refs[i][zone, :, r * HD : (r + 1) * HD] = o
            weight = jnp.where(lane == r, totals[sl], weight)
            top = jnp.where(lane == r, peak[sl], top)
        stats = _stats(top + jnp.log2(weight))
        o_refs[i][zone, :, REP * HD :] = stats.reshape(per, row_dev, HD)

    for i in range(n):
        for copy in copies[4 * i : 4 * i + 4]:
            copy.wait()
        peaks = [scores(i, h) for h in range(2)]
        for h in range(2):
            attend(i, h, peaks[h])


def _prompt(wanted, ids, qs, own, par):
    n = len(wanted)
    zs, row_dev, width = qs[0].shape
    span = own.shape[2]
    rows = zs // 2 * row_dev
    vmem = pl.BlockSpec(memory_space=pltpu.VMEM)
    hbm = pl.BlockSpec(memory_space=pltpu.HBM)
    anywhere = pl.BlockSpec(memory_space=pl.ANY)
    return pl.pallas_call(
        functools.partial(_prompt_kernel, wanted),
        out_shape=[jax.ShapeDtypeStruct((zs, row_dev, width + HD), BF16)] * n,
        in_specs=[vmem] * (n + 1) + [hbm, anywhere],
        out_specs=[vmem] * n,
        scratch_shapes=[
            pltpu.VMEM((n, 2, 2, 2 * span, 2 * HD), BF16),
            pltpu.VMEM((2, rows * REP, 2 * span), F32),
            pltpu.SemaphoreType.DMA((4 * n,)),
        ],
        compiler_params=pltpu.CompilerParams(vmem_limit_bytes=VMEM_LIMIT),
        cost_estimate=pl.CostEstimate(
            flops=n * 2 * 2 * 2 * rows * REP * 2 * span * 2 * HD,
            bytes_accessed=n * 2 * 2 * 4 * span * HD * 2,
            transcendentals=n * 2 * rows * REP * 2 * span,
        ),
    )(ids, *qs, own, par)


def _lse(x):
    s = x.astype(F32)
    return s + pltpu.roll(s, HD - REP, 1) + pltpu.roll(s, HD - 2 * REP, 1)


def _weights(l2s):
    top = functools.reduce(jnp.maximum, l2s)
    es = [jnp.exp2(l2 - top) for l2 in l2s]
    total = functools.reduce(jnp.add, es)
    return [e / total for e in es], top + jnp.log2(total)


def _merge_kernel(*all_refs):
    *refs, o_ref = all_refs
    lead = o_ref.shape[:2]
    rows = lead[0] * lead[1]
    lane = lax.broadcasted_iota(jnp.int32, (rows, HD), 1)
    l2s = [_lse(ref[:, :, REP * HD :].reshape(rows, HD)) for ref in refs]
    l2s = [jnp.where(lane < REP, x, 0.0) for x in l2s]
    ws, l2 = _weights(l2s)
    for r in range(REP):
        acc = None
        for w, ref in zip(ws, refs):
            x = ref[:, :, r * HD : (r + 1) * HD].reshape(rows, HD).astype(F32)
            x = x * w[:, r : r + 1]
            acc = x if acc is None else acc + x
        o_ref[:, :, r * HD : (r + 1) * HD] = acc.astype(BF16).reshape(*lead, HD)
    o_ref[:, :, REP * HD :] = _stats(l2).reshape(*lead, HD)


def _merge(parts):
    return pl.pallas_call(
        _merge_kernel,
        out_shape=jax.ShapeDtypeStruct(parts[0].shape, BF16),
        compiler_params=pltpu.CompilerParams(vmem_limit_bytes=VMEM_LIMIT),
    )(*parts)


def _final_kernel(p_ref, so_ref, sl_ref, o_ref):
    n = p_ref.shape[0]
    rows = p_ref.shape[1]
    lane = lax.broadcasted_iota(jnp.int32, (rows, HD), 1)
    l2s = [_lse(p_ref[i, :, REP * HD :]) for i in range(n)] + [sl_ref[...]]
    ws, _ = _weights([jnp.where(lane < REP, x, 0.0) for x in l2s])
    for r in range(REP):
        sl = slice(r * HD, (r + 1) * HD)
        acc = so_ref[:, sl] * ws[n][:, r : r + 1]
        for i in range(n):
            acc += p_ref[i, :, sl].astype(F32) * ws[i][:, r : r + 1]
        o_ref[:, sl] = acc.astype(BF16)


def _final(parts, suffix_o, suffix_l2):
    return pl.pallas_call(
        _final_kernel,
        out_shape=jax.ShapeDtypeStruct(suffix_o.shape, BF16),
        compiler_params=pltpu.CompilerParams(vmem_limit_bytes=VMEM_LIMIT),
    )(parts, suffix_o, suffix_l2)


def _suffix(q, kv, lengths):
    rows, suf = kv.shape[0], kv.shape[1]
    own_q = q.reshape(rows, REP, HD)
    scores = jnp.einsum("rhd,rsd->rhs", own_q, kv[:, :, 0], preferred_element_type=F32) * C2
    valid = jnp.arange(suf, dtype=jnp.int32)[None, None, :] < lengths[:, None, None]
    scores = jnp.where(valid, scores, -BIG)
    peak = jnp.max(scores, axis=2, keepdims=True)
    probs = jnp.exp2(scores - peak)
    total = jnp.sum(probs, axis=2)
    numer = jnp.einsum("rhs,rsd->rhd", probs.astype(BF16), kv[:, :, 1], preferred_element_type=F32)
    o = (numer / total[:, :, None]).reshape(rows, REP * HD)
    l2 = jnp.pad(peak[:, :, 0] + jnp.log2(total), ((0, 0), (0, HD - REP)))
    return o, l2


def _pairs(which):
    out = []
    for y in range(4):
        for core in range(2):
            to = 3 - y if (which == 1) == (core == 1) else y ^ 1
            out.append((2 * y + core, 2 * to + core))
    return out


def _shards(queries, prompt_kv, suffix_kv, suffix_len, group_of):
    q = queries[0]
    own = jnp.transpose(prompt_kv[0], (0, 2, 1, 3))

    n_z = lax.axis_size("zh") * lax.axis_size("zl")
    spread = jnp.broadcast_to(q[None], (n_z, *q.shape))
    q0 = lax.all_to_all(spread, ("zh", "zl"), 0, 0, tiled=True)
    q0, own = lax.optimization_barrier((q0, own))
    par = lax.ppermute(own, "core", [(0, 1), (1, 0)])
    first = lax.ppermute(q0, ("y", "core"), _pairs(1))
    first, q0 = lax.optimization_barrier((first, q0))
    third = lax.ppermute(first, ("y", "core"), _pairs(2))
    second = lax.ppermute(q0, ("y", "core"), _pairs(2))

    def part(which, block):
        return _prompt((which,), group_of, [block], own, par)[0]

    back_third = lax.ppermute(part(3, third), ("y", "core"), _pairs(2))
    part_second, part_first = lax.optimization_barrier((part(2, second), part(1, first)))
    back_second = lax.ppermute(part_second, ("y", "core"), _pairs(2))
    merged = _merge([part_first, back_third])
    back_first = lax.ppermute(merged, ("y", "core"), _pairs(1))
    merged = _merge([part(0, q0), back_second, back_first])
    merged, q, suffix_kv, suffix_len = lax.optimization_barrier(
        (merged, q, suffix_kv, suffix_len)
    )
    suffix_o, suffix_l2 = _suffix(q, suffix_kv[0], suffix_len[0])
    got = lax.all_to_all(merged, ("zh", "zl"), 0, 0, tiled=True)
    return _final(got, suffix_o, suffix_l2)[None]


def solution(mesh):
    fine = Mesh(
        np.asarray(mesh.devices).reshape(4, 2, 4, 2, 4), ("y", "zh", "zl", "core", "grp")
    )
    ctx, dec = ("y", "zh"), ("zl", "core")
    placed = (
        P("grp", dec, ctx),
        P("grp", None, ctx + dec, None, None),
        P("grp", dec, None, None, ctx),
        P("grp", dec),
        P("grp", None),
    )
    return jax.shard_map(
        _shards, mesh=fine, in_specs=placed, out_specs=P("grp", dec, ctx), check_vma=False
    )
```

```python
import functools
import math

import jax
import jax.numpy as jnp
import numpy as np
from jax import lax
from jax.experimental import pallas as pl
from jax.experimental.pallas import tpu as pltpu
from jax.sharding import Mesh
from jax.sharding import PartitionSpec as P

HD = 128
REP = 8
C2 = HD ** (-0.5) * math.log2(math.e)
BIG = 1e30
VMEM_LIMIT = 28 * 2**20
F32 = jnp.float32
BF16 = jnp.bfloat16


def _dot_t(a, b):
    return lax.dot_general(a, b, (((1,), (1,)), ((), ())), preferred_element_type=F32)


def _pack(l2):
    hi = l2.astype(BF16).astype(F32)
    rest = l2 - hi
    mid = rest.astype(BF16).astype(F32)
    return hi, mid, rest - mid


def _stats(l2):
    lane = lax.broadcasted_iota(jnp.int32, l2.shape, 1)
    hi, mid, lo = _pack(jnp.where(lane < REP, l2, 0.0))
    return (hi + pltpu.roll(mid, REP, 1) + pltpu.roll(lo, 2 * REP, 1)).astype(BF16)


def _partners(y, core):
    a, b = y + 1 - 2 * lax.rem(y, 2), 3 - y
    return y, jnp.where(core == 0, a, b), jnp.where(core == 0, b, a), lax.rem(y + 2, 4)


def _prompt_kernel(wanted, ids_ref, *refs):
    n = len(wanted)
    q_refs, (own_hbm, par_hbm), o_refs = refs[:n], refs[n : n + 2], refs[n + 2 : 2 * n + 2]
    kv_ref, s_ref, sem = refs[2 * n + 2 :]
    zs, row_dev = q_refs[0].shape[:2]
    per = zs // 2
    rows = per * row_dev
    span = own_hbm.shape[2]
    width = 2 * HD
    core = lax.axis_index("core")
    partners = _partners(lax.axis_index("y"), core)
    copies = []
    for i, partner in enumerate(wanted):
        at = pl.multiple_of(partners[partner] * width, width)
        for which in range(2):
            for k, ref in enumerate((own_hbm, par_hbm)):
                copy = pltpu.make_async_copy(
                    ref.at[:, which, :, pl.ds(at, width)],
                    kv_ref.at[i, which, :, pl.ds(k * span, span), :],
                    sem.at[len(copies)],
                )
                copy.start()
                copies.append(copy)

    total = ids_ref.shape[1]
    shape = (per, row_dev, total)
    source = lax.broadcasted_iota(jnp.int32, shape, 0) * (2 * row_dev)
    source += core * row_dev + lax.broadcasted_iota(jnp.int32, shape, 1)
    source = source.reshape(rows, total)
    lane = lax.broadcasted_iota(jnp.int32, (rows, total), 1)
    ids = jnp.broadcast_to(ids_ref[...].astype(F32), (rows, total))
    member = jnp.sum(jnp.where(lane == source, ids, 0.0), axis=1, keepdims=True)
    member = jnp.broadcast_to(member, (rows, HD))
    lane = lax.broadcasted_iota(jnp.int32, (rows, HD), 1)
    keep = ((1.0 - member).astype(BF16), member.astype(BF16))

    def scores(i, h):
        q = q_refs[i][h * per : (h + 1) * per].reshape(rows, REP * HD)
        lanes = slice(h * HD, (h + 1) * HD)
        k = jnp.concatenate([kv_ref[i, 0, 0, :, lanes], kv_ref[i, 0, 1, :, lanes]], axis=1)
        tops = []
        half = REP // 2
        for part in range(2):
            block = [q[:, r * HD : (r + 1) * HD] for r in range(part * half, (part + 1) * half)]
            block = [jnp.concatenate([x * keep[0], x * keep[1]], axis=1) for x in block]
            s = _dot_t(jnp.concatenate(block, axis=0), k)
            s_ref[h, part * half * rows : (part + 1) * half * rows] = s
            tops.append(jnp.max(s, axis=1, keepdims=True) * C2)
        return jnp.concatenate(tops, axis=0)

    def attend(i, h, peak):
        w = jnp.exp2(s_ref[h] * C2 - peak)
        totals = jnp.sum(w, axis=1, keepdims=True)
        lanes = slice(h * HD, (h + 1) * HD)
        v = jnp.concatenate([kv_ref[i, 1, 0, :, lanes], kv_ref[i, 1, 1, :, lanes]], axis=1)
        acc = jnp.dot(w.astype(BF16), v, preferred_element_type=F32)
        inverse = 1.0 / totals
        weight = jnp.ones((rows, HD), F32)
        top = jnp.zeros((rows, HD), F32)
        zone = slice(h * per, (h + 1) * per)
        for r in range(REP):
            sl = slice(r * rows, (r + 1) * rows)
            o = jnp.where(member > 0.5, acc[sl, HD:], acc[sl, :HD]) * inverse[sl]
            o = o.astype(BF16).reshape(per, row_dev, HD)
            o_refs[i][zone, :, r * HD : (r + 1) * HD] = o
            weight = jnp.where(lane == r, totals[sl], weight)
            top = jnp.where(lane == r, peak[sl], top)
        stats = _stats(top + jnp.log2(weight))
        o_refs[i][zone, :, REP * HD :] = stats.reshape(per, row_dev, HD)

    for i in range(n):
        for copy in copies[4 * i : 4 * i + 4]:
            copy.wait()
        peaks = [scores(i, h) for h in range(2)]
        for h in range(2):
            attend(i, h, peaks[h])


def _prompt(wanted, ids, qs, own, par):
    n = len(wanted)
    zs, row_dev, width = qs[0].shape
    span = own.shape[2]
    rows = zs // 2 * row_dev
    vmem = pl.BlockSpec(memory_space=pltpu.VMEM)
    hbm = pl.BlockSpec(memory_space=pltpu.HBM)
    anywhere = pl.BlockSpec(memory_space=pl.ANY)
    return pl.pallas_call(
        functools.partial(_prompt_kernel, wanted),
        out_shape=[jax.ShapeDtypeStruct((zs, row_dev, width + HD), BF16)] * n,
        in_specs=[vmem] * (n + 1) + [hbm, anywhere],
        out_specs=[vmem] * n,
        scratch_shapes=[
            pltpu.VMEM((n, 2, 2, 2 * span, 2 * HD), BF16),
            pltpu.VMEM((2, rows * REP, 2 * span), F32),
            pltpu.SemaphoreType.DMA((4 * n,)),
        ],
        compiler_params=pltpu.CompilerParams(vmem_limit_bytes=VMEM_LIMIT),
        cost_estimate=pl.CostEstimate(
            flops=n * 2 * 2 * 2 * rows * REP * 2 * span * 2 * HD,
            bytes_accessed=n * 2 * 2 * 4 * span * HD * 2,
            transcendentals=n * 2 * rows * REP * 2 * span,
        ),
    )(ids, *qs, own, par)


def _lse(x):
    s = x.astype(F32)
    return s + pltpu.roll(s, HD - REP, 1) + pltpu.roll(s, HD - 2 * REP, 1)


def _weights(l2s):
    top = functools.reduce(jnp.maximum, l2s)
    es = [jnp.exp2(l2 - top) for l2 in l2s]
    total = functools.reduce(jnp.add, es)
    return [e / total for e in es], top + jnp.log2(total)


def _merge_kernel(*all_refs):
    *refs, o_ref = all_refs
    lead = o_ref.shape[:2]
    rows = lead[0] * lead[1]
    lane = lax.broadcasted_iota(jnp.int32, (rows, HD), 1)
    l2s = [_lse(ref[:, :, REP * HD :].reshape(rows, HD)) for ref in refs]
    l2s = [jnp.where(lane < REP, x, 0.0) for x in l2s]
    ws, l2 = _weights(l2s)
    for r in range(REP):
        acc = None
        for w, ref in zip(ws, refs):
            x = ref[:, :, r * HD : (r + 1) * HD].reshape(rows, HD).astype(F32)
            x = x * w[:, r : r + 1]
            acc = x if acc is None else acc + x
        o_ref[:, :, r * HD : (r + 1) * HD] = acc.astype(BF16).reshape(*lead, HD)
    o_ref[:, :, REP * HD :] = _stats(l2).reshape(*lead, HD)


def _merge(parts):
    return pl.pallas_call(
        _merge_kernel,
        out_shape=jax.ShapeDtypeStruct(parts[0].shape, BF16),
        compiler_params=pltpu.CompilerParams(vmem_limit_bytes=VMEM_LIMIT),
    )(*parts)


def _final_kernel(p_ref, so_ref, sl_ref, o_ref):
    n = p_ref.shape[0]
    rows = p_ref.shape[1]
    lane = lax.broadcasted_iota(jnp.int32, (rows, HD), 1)
    l2s = [_lse(p_ref[i, :, REP * HD :]) for i in range(n)] + [sl_ref[...]]
    ws, _ = _weights([jnp.where(lane < REP, x, 0.0) for x in l2s])
    for r in range(REP):
        sl = slice(r * HD, (r + 1) * HD)
        acc = so_ref[:, sl] * ws[n][:, r : r + 1]
        for i in range(n):
            acc += p_ref[i, :, sl].astype(F32) * ws[i][:, r : r + 1]
        o_ref[:, sl] = acc.astype(BF16)


def _final(parts, suffix_o, suffix_l2):
    return pl.pallas_call(
        _final_kernel,
        out_shape=jax.ShapeDtypeStruct(suffix_o.shape, BF16),
        compiler_params=pltpu.CompilerParams(vmem_limit_bytes=VMEM_LIMIT),
    )(parts, suffix_o, suffix_l2)


def _suffix(q, kv, lengths):
    rows, suf = kv.shape[0], kv.shape[1]
    own_q = q.reshape(rows, REP, HD)
    scores = jnp.einsum("rhd,rsd->rhs", own_q, kv[:, :, 0], preferred_element_type=F32) * C2
    valid = jnp.arange(suf, dtype=jnp.int32)[None, None, :] < lengths[:, None, None]
    scores = jnp.where(valid, scores, -BIG)
    peak = jnp.max(scores, axis=2, keepdims=True)
    probs = jnp.exp2(scores - peak)
    total = jnp.sum(probs, axis=2)
    numer = jnp.einsum("rhs,rsd->rhd", probs.astype(BF16), kv[:, :, 1], preferred_element_type=F32)
    o = (numer / total[:, :, None]).reshape(rows, REP * HD)
    l2 = jnp.pad(peak[:, :, 0] + jnp.log2(total), ((0, 0), (0, HD - REP)))
    return o, l2


def _pairs(which):
    out = []
    for y in range(4):
        for core in range(2):
            to = 3 - y if (which == 1) == (core == 1) else y ^ 1
            out.append((2 * y + core, 2 * to + core))
    return out


def _shards(queries, prompt_kv, suffix_kv, suffix_len, group_of):
    q = queries[0]
    own = jnp.transpose(prompt_kv[0], (0, 2, 1, 3))

    n_z = lax.axis_size("zh") * lax.axis_size("zl")
    spread = jnp.broadcast_to(q[None], (n_z, *q.shape))
    q0 = lax.all_to_all(spread, ("zh", "zl"), 0, 0, tiled=True)
    q0, own = lax.optimization_barrier((q0, own))
    par = lax.ppermute(own, "core", [(0, 1), (1, 0)])
    first = lax.ppermute(q0, ("y", "core"), _pairs(1))
    first, q0 = lax.optimization_barrier((first, q0))
    third = lax.ppermute(first, ("y", "core"), _pairs(2))
    q0, par = lax.optimization_barrier((q0, par))
    second = lax.ppermute(q0, ("y", "core"), _pairs(2))

    def part(which, block):
        return _prompt((which,), group_of, [block], own, par)[0]

    part_first, third = lax.optimization_barrier((part(1, first), third))
    back_third = lax.ppermute(part(3, third), ("y", "core"), _pairs(2))
    back_second = lax.ppermute(part(2, second), ("y", "core"), _pairs(2))
    merged = _merge([part_first, back_third])
    back_first = lax.ppermute(merged, ("y", "core"), _pairs(1))
    merged = _merge([part(0, q0), back_second, back_first])
    merged, q, suffix_kv, suffix_len = lax.optimization_barrier(
        (merged, q, suffix_kv, suffix_len)
    )
    suffix_o, suffix_l2 = _suffix(q, suffix_kv[0], suffix_len[0])
    got = lax.all_to_all(merged, ("zh", "zl"), 0, 0, tiled=True)
    return _final(got, suffix_o, suffix_l2)[None]


def solution(mesh):
    fine = Mesh(
        np.asarray(mesh.devices).reshape(4, 2, 4, 2, 4), ("y", "zh", "zl", "core", "grp")
    )
    ctx, dec = ("y", "zh"), ("zl", "core")
    placed = (
        P("grp", dec, ctx),
        P("grp", None, ctx + dec, None, None),
        P("grp", dec, None, None, ctx),
        P("grp", dec),
        P("grp", None),
    )
    return jax.shard_map(
        _shards, mesh=fine, in_specs=placed, out_specs=P("grp", dec, ctx), check_vma=False
    )
```

```python
import functools
import math

import jax
import jax.numpy as jnp
import numpy as np
from jax import lax
from jax.experimental import pallas as pl
from jax.experimental.pallas import tpu as pltpu
from jax.sharding import Mesh
from jax.sharding import PartitionSpec as P

HD = 128
REP = 8
C2 = HD ** (-0.5) * math.log2(math.e)
BIG = 1e30
VMEM_LIMIT = 28 * 2**20
F32 = jnp.float32
BF16 = jnp.bfloat16


def _dot_t(a, b):
    return lax.dot_general(a, b, (((1,), (1,)), ((), ())), preferred_element_type=F32)


def _pack(l2):
    hi = l2.astype(BF16).astype(F32)
    rest = l2 - hi
    mid = rest.astype(BF16).astype(F32)
    return hi, mid, rest - mid


def _stats(l2):
    lane = lax.broadcasted_iota(jnp.int32, l2.shape, 1)
    hi, mid, lo = _pack(jnp.where(lane < REP, l2, 0.0))
    return (hi + pltpu.roll(mid, REP, 1) + pltpu.roll(lo, 2 * REP, 1)).astype(BF16)


def _partners(y, core):
    a, b = y + 1 - 2 * lax.rem(y, 2), 3 - y
    return y, jnp.where(core == 0, a, b), jnp.where(core == 0, b, a), lax.rem(y + 2, 4)


def _prompt_kernel(wanted, ids_ref, *refs):
    n = len(wanted)
    q_refs, (own_hbm, par_hbm), o_refs = refs[:n], refs[n : n + 2], refs[n + 2 : 2 * n + 2]
    kv_ref, s_ref, sem = refs[2 * n + 2 :]
    zs, row_dev = q_refs[0].shape[:2]
    per = zs // 2
    rows = per * row_dev
    span = own_hbm.shape[2]
    width = 2 * HD
    core = lax.axis_index("core")
    partners = _partners(lax.axis_index("y"), core)
    copies = []
    for i, partner in enumerate(wanted):
        at = pl.multiple_of(partners[partner] * width, width)
        for which in range(2):
            for k, ref in enumerate((own_hbm, par_hbm)):
                copy = pltpu.make_async_copy(
                    ref.at[:, which, :, pl.ds(at, width)],
                    kv_ref.at[i, which, :, pl.ds(k * span, span), :],
                    sem.at[len(copies)],
                )
                copy.start()
                copies.append(copy)

    total = ids_ref.shape[1]
    shape = (per, row_dev, total)
    source = lax.broadcasted_iota(jnp.int32, shape, 0) * (2 * row_dev)
    source += core * row_dev + lax.broadcasted_iota(jnp.int32, shape, 1)
    source = source.reshape(rows, total)
    lane = lax.broadcasted_iota(jnp.int32, (rows, total), 1)
    ids = jnp.broadcast_to(ids_ref[...].astype(F32), (rows, total))
    member = jnp.sum(jnp.where(lane == source, ids, 0.0), axis=1, keepdims=True)
    member = jnp.broadcast_to(member, (rows, HD))
    lane = lax.broadcasted_iota(jnp.int32, (rows, HD), 1)
    keep = ((1.0 - member).astype(BF16), member.astype(BF16))

    def scores(i, h):
        q = q_refs[i][h * per : (h + 1) * per].reshape(rows, REP * HD)
        lanes = slice(h * HD, (h + 1) * HD)
        k = jnp.concatenate([kv_ref[i, 0, 0, :, lanes], kv_ref[i, 0, 1, :, lanes]], axis=1)
        tops = []
        half = REP // 2
        for part in range(2):
            block = [q[:, r * HD : (r + 1) * HD] for r in range(part * half, (part + 1) * half)]
            block = [jnp.concatenate([x * keep[0], x * keep[1]], axis=1) for x in block]
            s = _dot_t(jnp.concatenate(block, axis=0), k)
            s_ref[h, part * half * rows : (part + 1) * half * rows] = s
            tops.append(jnp.max(s, axis=1, keepdims=True) * C2)
        return jnp.concatenate(tops, axis=0)

    def attend(i, h, peak):
        w = jnp.exp2(s_ref[h] * C2 - peak)
        totals = jnp.sum(w, axis=1, keepdims=True)
        lanes = slice(h * HD, (h + 1) * HD)
        v = jnp.concatenate([kv_ref[i, 1, 0, :, lanes], kv_ref[i, 1, 1, :, lanes]], axis=1)
        acc = jnp.dot(w.astype(BF16), v, preferred_element_type=F32)
        inverse = 1.0 / totals
        weight = jnp.ones((rows, HD), F32)
        top = jnp.zeros((rows, HD), F32)
        zone = slice(h * per, (h + 1) * per)
        for r in range(REP):
            sl = slice(r * rows, (r + 1) * rows)
            o = jnp.where(member > 0.5, acc[sl, HD:], acc[sl, :HD]) * inverse[sl]
            o = o.astype(BF16).reshape(per, row_dev, HD)
            o_refs[i][zone, :, r * HD : (r + 1) * HD] = o
            weight = jnp.where(lane == r, totals[sl], weight)
            top = jnp.where(lane == r, peak[sl], top)
        stats = _stats(top + jnp.log2(weight))
        o_refs[i][zone, :, REP * HD :] = stats.reshape(per, row_dev, HD)

    for i in range(n):
        for copy in copies[4 * i : 4 * i + 4]:
            copy.wait()
        peaks = [scores(i, h) for h in range(2)]
        for h in range(2):
            attend(i, h, peaks[h])


def _prompt(wanted, ids, qs, own, par):
    n = len(wanted)
    zs, row_dev, width = qs[0].shape
    span = own.shape[2]
    rows = zs // 2 * row_dev
    vmem = pl.BlockSpec(memory_space=pltpu.VMEM)
    hbm = pl.BlockSpec(memory_space=pltpu.HBM)
    anywhere = pl.BlockSpec(memory_space=pl.ANY)
    return pl.pallas_call(
        functools.partial(_prompt_kernel, wanted),
        out_shape=[jax.ShapeDtypeStruct((zs, row_dev, width + HD), BF16)] * n,
        in_specs=[vmem] * (n + 1) + [hbm, anywhere],
        out_specs=[vmem] * n,
        scratch_shapes=[
            pltpu.VMEM((n, 2, 2, 2 * span, 2 * HD), BF16),
            pltpu.VMEM((2, rows * REP, 2 * span), F32),
            pltpu.SemaphoreType.DMA((4 * n,)),
        ],
        compiler_params=pltpu.CompilerParams(vmem_limit_bytes=VMEM_LIMIT),
        cost_estimate=pl.CostEstimate(
            flops=n * 2 * 2 * 2 * rows * REP * 2 * span * 2 * HD,
            bytes_accessed=n * 2 * 2 * 4 * span * HD * 2,
            transcendentals=n * 2 * rows * REP * 2 * span,
        ),
    )(ids, *qs, own, par)


def _lse(x):
    s = x.astype(F32)
    return s + pltpu.roll(s, HD - REP, 1) + pltpu.roll(s, HD - 2 * REP, 1)


def _weights(l2s):
    top = functools.reduce(jnp.maximum, l2s)
    es = [jnp.exp2(l2 - top) for l2 in l2s]
    total = functools.reduce(jnp.add, es)
    return [e / total for e in es], top + jnp.log2(total)


def _merge_kernel(*all_refs):
    *refs, o_ref = all_refs
    lead = o_ref.shape[:2]
    rows = lead[0] * lead[1]
    lane = lax.broadcasted_iota(jnp.int32, (rows, HD), 1)
    l2s = [_lse(ref[:, :, REP * HD :].reshape(rows, HD)) for ref in refs]
    l2s = [jnp.where(lane < REP, x, 0.0) for x in l2s]
    ws, l2 = _weights(l2s)
    for r in range(REP):
        acc = None
        for w, ref in zip(ws, refs):
            x = ref[:, :, r * HD : (r + 1) * HD].reshape(rows, HD).astype(F32)
            x = x * w[:, r : r + 1]
            acc = x if acc is None else acc + x
        o_ref[:, :, r * HD : (r + 1) * HD] = acc.astype(BF16).reshape(*lead, HD)
    o_ref[:, :, REP * HD :] = _stats(l2).reshape(*lead, HD)


def _merge(parts):
    return pl.pallas_call(
        _merge_kernel,
        out_shape=jax.ShapeDtypeStruct(parts[0].shape, BF16),
        compiler_params=pltpu.CompilerParams(vmem_limit_bytes=VMEM_LIMIT),
    )(*parts)


def _final_kernel(p_ref, so_ref, sl_ref, o_ref):
    n = p_ref.shape[0]
    rows = p_ref.shape[1]
    lane = lax.broadcasted_iota(jnp.int32, (rows, HD), 1)
    l2s = [_lse(p_ref[i, :, REP * HD :]) for i in range(n)] + [sl_ref[...]]
    ws, _ = _weights([jnp.where(lane < REP, x, 0.0) for x in l2s])
    for r in range(REP):
        sl = slice(r * HD, (r + 1) * HD)
        acc = so_ref[:, sl] * ws[n][:, r : r + 1]
        for i in range(n):
            acc += p_ref[i, :, sl].astype(F32) * ws[i][:, r : r + 1]
        o_ref[:, sl] = acc.astype(BF16)


def _final(parts, suffix_o, suffix_l2):
    return pl.pallas_call(
        _final_kernel,
        out_shape=jax.ShapeDtypeStruct(suffix_o.shape, BF16),
        compiler_params=pltpu.CompilerParams(vmem_limit_bytes=VMEM_LIMIT),
    )(parts, suffix_o, suffix_l2)


def _suffix(q, kv, lengths):
    rows, suf = kv.shape[0], kv.shape[1]
    own_q = q.reshape(rows, REP, HD)
    scores = jnp.einsum("rhd,rsd->rhs", own_q, kv[:, :, 0], preferred_element_type=F32) * C2
    valid = jnp.arange(suf, dtype=jnp.int32)[None, None, :] < lengths[:, None, None]
    scores = jnp.where(valid, scores, -BIG)
    peak = jnp.max(scores, axis=2, keepdims=True)
    probs = jnp.exp2(scores - peak)
    total = jnp.sum(probs, axis=2)
    numer = jnp.einsum("rhs,rsd->rhd", probs.astype(BF16), kv[:, :, 1], preferred_element_type=F32)
    o = (numer / total[:, :, None]).reshape(rows, REP * HD)
    l2 = jnp.pad(peak[:, :, 0] + jnp.log2(total), ((0, 0), (0, HD - REP)))
    return o, l2


def _pairs(which):
    out = []
    for y in range(4):
        for core in range(2):
            to = 3 - y if (which == 1) == (core == 1) else y ^ 1
            out.append((2 * y + core, 2 * to + core))
    return out


def _shards(queries, prompt_kv, suffix_kv, suffix_len, group_of):
    q = queries[0]
    own = jnp.transpose(prompt_kv[0], (0, 2, 1, 3))

    n_z = lax.axis_size("zh") * lax.axis_size("zl")
    spread = jnp.broadcast_to(q[None], (n_z, *q.shape))
    q0 = lax.all_to_all(spread, ("zh", "zl"), 0, 0, tiled=True)
    q0, own = lax.optimization_barrier((q0, own))
    par = lax.ppermute(own, "core", [(0, 1), (1, 0)])
    first = lax.ppermute(q0, ("y", "core"), _pairs(1))
    first, q0 = lax.optimization_barrier((first, q0))
    third = lax.ppermute(first, ("y", "core"), _pairs(2))
    second = lax.ppermute(q0, ("y", "core"), _pairs(2))

    def part(which, block):
        return _prompt((which,), group_of, [block], own, par)[0]

    part_first, third = lax.optimization_barrier((part(1, first), third))
    back_third = lax.ppermute(part(3, third), ("y", "core"), _pairs(2))
    back_second = lax.ppermute(part(2, second), ("y", "core"), _pairs(2))
    merged = _merge([part_first, back_third])
    back_first = lax.ppermute(merged, ("y", "core"), _pairs(1))
    merged = _merge([part(0, q0), back_second, back_first])
    merged, q, suffix_kv, suffix_len = lax.optimization_barrier(
        (merged, q, suffix_kv, suffix_len)
    )
    suffix_o, suffix_l2 = _suffix(q, suffix_kv[0], suffix_len[0])
    got = lax.all_to_all(merged, ("zh", "zl"), 0, 0, tiled=True)
    return _final(got, suffix_o, suffix_l2)[None]


def solution(mesh):
    fine = Mesh(
        np.asarray(mesh.devices).reshape(4, 2, 4, 2, 4), ("y", "zh", "zl", "core", "grp")
    )
    ctx, dec = ("y", "zh"), ("zl", "core")
    placed = (
        P("grp", dec, ctx),
        P("grp", None, ctx + dec, None, None),
        P("grp", dec, None, None, ctx),
        P("grp", dec),
        P("grp", None),
    )
    return jax.shard_map(
        _shards, mesh=fine, in_specs=placed, out_specs=P("grp", dec, ctx), check_vma=False
    )
```

```python
import functools
import math

import jax
import jax.numpy as jnp
import numpy as np
from jax import lax
from jax.experimental import pallas as pl
from jax.experimental.pallas import tpu as pltpu
from jax.sharding import Mesh
from jax.sharding import PartitionSpec as P

HD = 128
REP = 8
C2 = HD ** (-0.5) * math.log2(math.e)
BIG = 1e30
VMEM_LIMIT = 28 * 2**20
F32 = jnp.float32
BF16 = jnp.bfloat16


def _dot_t(a, b):
    return lax.dot_general(a, b, (((1,), (1,)), ((), ())), preferred_element_type=F32)


def _pack(l2):
    hi = l2.astype(BF16).astype(F32)
    rest = l2 - hi
    mid = rest.astype(BF16).astype(F32)
    return hi, mid, rest - mid


def _stats(l2):
    lane = lax.broadcasted_iota(jnp.int32, l2.shape, 1)
    hi, mid, lo = _pack(jnp.where(lane < REP, l2, 0.0))
    return (hi + pltpu.roll(mid, REP, 1) + pltpu.roll(lo, 2 * REP, 1)).astype(BF16)


def _partners(y, core):
    a, b = y + 1 - 2 * lax.rem(y, 2), 3 - y
    return y, jnp.where(core == 0, a, b), jnp.where(core == 0, b, a), lax.rem(y + 2, 4)


def _prompt_kernel(wanted, ids_ref, *refs):
    n = len(wanted)
    q_refs, (own_hbm, par_hbm), o_refs = refs[:n], refs[n : n + 2], refs[n + 2 : 2 * n + 2]
    kv_ref, s_ref, sem = refs[2 * n + 2 :]
    zs, row_dev = q_refs[0].shape[:2]
    per = zs // 2
    rows = per * row_dev
    span = own_hbm.shape[2]
    width = 2 * HD
    core = lax.axis_index("core")
    partners = _partners(lax.axis_index("y"), core)
    copies = []
    for i, partner in enumerate(wanted):
        at = pl.multiple_of(partners[partner] * width, width)
        for which in range(2):
            for k, ref in enumerate((own_hbm, par_hbm)):
                copy = pltpu.make_async_copy(
                    ref.at[:, which, :, pl.ds(at, width)],
                    kv_ref.at[i, which, :, pl.ds(k * span, span), :],
                    sem.at[len(copies)],
                )
                copy.start()
                copies.append(copy)

    total = ids_ref.shape[1]
    shape = (per, row_dev, total)
    source = lax.broadcasted_iota(jnp.int32, shape, 0) * (2 * row_dev)
    source += core * row_dev + lax.broadcasted_iota(jnp.int32, shape, 1)
    source = source.reshape(rows, total)
    lane = lax.broadcasted_iota(jnp.int32, (rows, total), 1)
    ids = jnp.broadcast_to(ids_ref[...].astype(F32), (rows, total))
    member = jnp.sum(jnp.where(lane == source, ids, 0.0), axis=1, keepdims=True)
    member = jnp.broadcast_to(member, (rows, HD))
    lane = lax.broadcasted_iota(jnp.int32, (rows, HD), 1)
    keep = ((1.0 - member).astype(BF16), member.astype(BF16))

    def scores(i, h):
        q = q_refs[i][h * per : (h + 1) * per].reshape(rows, REP * HD)
        lanes = slice(h * HD, (h + 1) * HD)
        k = jnp.concatenate([kv_ref[i, 0, 0, :, lanes], kv_ref[i, 0, 1, :, lanes]], axis=1)
        tops = []
        half = REP // 2
        for part in range(2):
            block = [q[:, r * HD : (r + 1) * HD] for r in range(part * half, (part + 1) * half)]
            block = [jnp.concatenate([x * keep[0], x * keep[1]], axis=1) for x in block]
            s = _dot_t(jnp.concatenate(block, axis=0), k)
            s_ref[h, part * half * rows : (part + 1) * half * rows] = s
            tops.append(jnp.max(s, axis=1, keepdims=True) * C2)
        return jnp.concatenate(tops, axis=0)

    def attend(i, h, peak):
        w = jnp.exp2(s_ref[h] * C2 - peak)
        totals = jnp.sum(w, axis=1, keepdims=True)
        lanes = slice(h * HD, (h + 1) * HD)
        v = jnp.concatenate([kv_ref[i, 1, 0, :, lanes], kv_ref[i, 1, 1, :, lanes]], axis=1)
        acc = jnp.dot(w.astype(BF16), v, preferred_element_type=F32)
        inverse = 1.0 / totals
        weight = jnp.ones((rows, HD), F32)
        top = jnp.zeros((rows, HD), F32)
        zone = slice(h * per, (h + 1) * per)
        for r in range(REP):
            sl = slice(r * rows, (r + 1) * rows)
            o = jnp.where(member > 0.5, acc[sl, HD:], acc[sl, :HD]) * inverse[sl]
            o = o.astype(BF16).reshape(per, row_dev, HD)
            o_refs[i][zone, :, r * HD : (r + 1) * HD] = o
            weight = jnp.where(lane == r, totals[sl], weight)
            top = jnp.where(lane == r, peak[sl], top)
        stats = _stats(top + jnp.log2(weight))
        o_refs[i][zone, :, REP * HD :] = stats.reshape(per, row_dev, HD)

    for i in range(n):
        for copy in copies[4 * i : 4 * i + 4]:
            copy.wait()
        peaks = [scores(i, h) for h in range(2)]
        for h in range(2):
            attend(i, h, peaks[h])


def _prompt(wanted, ids, qs, own, par):
    n = len(wanted)
    zs, row_dev, width = qs[0].shape
    span = own.shape[2]
    rows = zs // 2 * row_dev
    vmem = pl.BlockSpec(memory_space=pltpu.VMEM)
    hbm = pl.BlockSpec(memory_space=pltpu.HBM)
    anywhere = pl.BlockSpec(memory_space=pl.ANY)
    return pl.pallas_call(
        functools.partial(_prompt_kernel, wanted),
        out_shape=[jax.ShapeDtypeStruct((zs, row_dev, width + HD), BF16)] * n,
        in_specs=[vmem] * (n + 1) + [hbm, anywhere],
        out_specs=[vmem] * n,
        scratch_shapes=[
            pltpu.VMEM((n, 2, 2, 2 * span, 2 * HD), BF16),
            pltpu.VMEM((2, rows * REP, 2 * span), F32),
            pltpu.SemaphoreType.DMA((4 * n,)),
        ],
        compiler_params=pltpu.CompilerParams(vmem_limit_bytes=VMEM_LIMIT),
        cost_estimate=pl.CostEstimate(
            flops=n * 2 * 2 * 2 * rows * REP * 2 * span * 2 * HD,
            bytes_accessed=n * 2 * 2 * 4 * span * HD * 2,
            transcendentals=n * 2 * rows * REP * 2 * span,
        ),
    )(ids, *qs, own, par)


def _lse(x):
    s = x.astype(F32)
    return s + pltpu.roll(s, HD - REP, 1) + pltpu.roll(s, HD - 2 * REP, 1)


def _weights(l2s):
    top = functools.reduce(jnp.maximum, l2s)
    es = [jnp.exp2(l2 - top) for l2 in l2s]
    total = functools.reduce(jnp.add, es)
    return [e / total for e in es], top + jnp.log2(total)


def _merge_kernel(*all_refs):
    *refs, o_ref = all_refs
    lead = o_ref.shape[:2]
    rows = lead[0] * lead[1]
    lane = lax.broadcasted_iota(jnp.int32, (rows, HD), 1)
    l2s = [_lse(ref[:, :, REP * HD :].reshape(rows, HD)) for ref in refs]
    l2s = [jnp.where(lane < REP, x, 0.0) for x in l2s]
    ws, l2 = _weights(l2s)
    for r in range(REP):
        acc = None
        for w, ref in zip(ws, refs):
            x = ref[:, :, r * HD : (r + 1) * HD].reshape(rows, HD).astype(F32)
            x = x * w[:, r : r + 1]
            acc = x if acc is None else acc + x
        o_ref[:, :, r * HD : (r + 1) * HD] = acc.astype(BF16).reshape(*lead, HD)
    o_ref[:, :, REP * HD :] = _stats(l2).reshape(*lead, HD)


def _merge(parts):
    return pl.pallas_call(
        _merge_kernel,
        out_shape=jax.ShapeDtypeStruct(parts[0].shape, BF16),
        compiler_params=pltpu.CompilerParams(vmem_limit_bytes=VMEM_LIMIT),
    )(*parts)


def _final_kernel(p_ref, so_ref, sl_ref, o_ref):
    n = p_ref.shape[0]
    rows = p_ref.shape[1]
    lane = lax.broadcasted_iota(jnp.int32, (rows, HD), 1)
    l2s = [_lse(p_ref[i, :, REP * HD :]) for i in range(n)] + [sl_ref[...]]
    ws, _ = _weights([jnp.where(lane < REP, x, 0.0) for x in l2s])
    for r in range(REP):
        sl = slice(r * HD, (r + 1) * HD)
        acc = so_ref[:, sl] * ws[n][:, r : r + 1]
        for i in range(n):
            acc += p_ref[i, :, sl].astype(F32) * ws[i][:, r : r + 1]
        o_ref[:, sl] = acc.astype(BF16)


def _final(parts, suffix_o, suffix_l2):
    return pl.pallas_call(
        _final_kernel,
        out_shape=jax.ShapeDtypeStruct(suffix_o.shape, BF16),
        compiler_params=pltpu.CompilerParams(vmem_limit_bytes=VMEM_LIMIT),
    )(parts, suffix_o, suffix_l2)


def _suffix(q, kv, lengths):
    rows, suf = kv.shape[0], kv.shape[1]
    own_q = q.reshape(rows, REP, HD)
    scores = jnp.einsum("rhd,rsd->rhs", own_q, kv[:, :, 0], preferred_element_type=F32) * C2
    valid = jnp.arange(suf, dtype=jnp.int32)[None, None, :] < lengths[:, None, None]
    scores = jnp.where(valid, scores, -BIG)
    peak = jnp.max(scores, axis=2, keepdims=True)
    probs = jnp.exp2(scores - peak)
    total = jnp.sum(probs, axis=2)
    numer = jnp.einsum("rhs,rsd->rhd", probs.astype(BF16), kv[:, :, 1], preferred_element_type=F32)
    o = (numer / total[:, :, None]).reshape(rows, REP * HD)
    l2 = jnp.pad(peak[:, :, 0] + jnp.log2(total), ((0, 0), (0, HD - REP)))
    return o, l2


def _pairs(which):
    out = []
    for y in range(4):
        for core in range(2):
            to = 3 - y if (which == 1) == (core == 1) else y ^ 1
            out.append((2 * y + core, 2 * to + core))
    return out


def _shards(queries, prompt_kv, suffix_kv, suffix_len, group_of):
    q = queries[0]
    own = jnp.transpose(prompt_kv[0], (0, 2, 1, 3))

    n_z = lax.axis_size("zh") * lax.axis_size("zl")
    spread = jnp.broadcast_to(q[None], (n_z, *q.shape))
    q0 = lax.all_to_all(spread, ("zh", "zl"), 0, 0, tiled=True)
    q0, own = lax.optimization_barrier((q0, own))
    par = lax.ppermute(own, "core", [(0, 1), (1, 0)])
    first = lax.ppermute(q0, ("y", "core"), _pairs(1))
    suffix_o, suffix_l2 = _suffix(q, suffix_kv[0], suffix_len[0])
    first, q0, suffix_o, suffix_l2 = lax.optimization_barrier((first, q0, suffix_o, suffix_l2))
    third = lax.ppermute(first, ("y", "core"), _pairs(2))
    second = lax.ppermute(q0, ("y", "core"), _pairs(2))

    def part(which, block):
        return _prompt((which,), group_of, [block], own, par)[0]

    part_first, third = lax.optimization_barrier((part(1, first), third))
    back_third = lax.ppermute(part(3, third), ("y", "core"), _pairs(2))
    back_second = lax.ppermute(part(2, second), ("y", "core"), _pairs(2))
    merged = _merge([part_first, back_third])
    back_first = lax.ppermute(merged, ("y", "core"), _pairs(1))
    merged = _merge([part(0, q0), back_second, back_first])
    got = lax.all_to_all(merged, ("zh", "zl"), 0, 0, tiled=True)
    return _final(got, suffix_o, suffix_l2)[None]


def solution(mesh):
    fine = Mesh(
        np.asarray(mesh.devices).reshape(4, 2, 4, 2, 4), ("y", "zh", "zl", "core", "grp")
    )
    ctx, dec = ("y", "zh"), ("zl", "core")
    placed = (
        P("grp", dec, ctx),
        P("grp", None, ctx + dec, None, None),
        P("grp", dec, None, None, ctx),
        P("grp", dec),
        P("grp", None),
    )
    return jax.shard_map(
        _shards, mesh=fine, in_specs=placed, out_specs=P("grp", dec, ctx), check_vma=False
    )
```

```python
import functools
import math

import jax
import jax.numpy as jnp
import numpy as np
from jax import lax
from jax.experimental import pallas as pl
from jax.experimental.pallas import tpu as pltpu
from jax.sharding import Mesh
from jax.sharding import PartitionSpec as P

HD = 128
REP = 8
C2 = HD ** (-0.5) * math.log2(math.e)
BIG = 1e30
VMEM_LIMIT = 28 * 2**20
F32 = jnp.float32
BF16 = jnp.bfloat16


def _dot_t(a, b):
    return lax.dot_general(a, b, (((1,), (1,)), ((), ())), preferred_element_type=F32)


def _pack(l2):
    hi = l2.astype(BF16).astype(F32)
    rest = l2 - hi
    mid = rest.astype(BF16).astype(F32)
    return hi, mid, rest - mid


def _stats(l2):
    lane = lax.broadcasted_iota(jnp.int32, l2.shape, 1)
    hi, mid, lo = _pack(jnp.where(lane < REP, l2, 0.0))
    return (hi + pltpu.roll(mid, REP, 1) + pltpu.roll(lo, 2 * REP, 1)).astype(BF16)


def _partners(y, core):
    a, b = y + 1 - 2 * lax.rem(y, 2), 3 - y
    return y, jnp.where(core == 0, a, b), jnp.where(core == 0, b, a), lax.rem(y + 2, 4)


def _prompt_kernel(wanted, ids_ref, *refs):
    n = len(wanted)
    q_refs, (own_hbm, par_hbm), o_refs = refs[:n], refs[n : n + 2], refs[n + 2 : 2 * n + 2]
    kv_ref, s_ref, sem = refs[2 * n + 2 :]
    zs, row_dev = q_refs[0].shape[:2]
    per = zs // 2
    rows = per * row_dev
    span = own_hbm.shape[2]
    width = 2 * HD
    core = lax.axis_index("core")
    partners = _partners(lax.axis_index("y"), core)
    copies = []
    for i, partner in enumerate(wanted):
        at = pl.multiple_of(partners[partner] * width, width)
        for which in range(2):
            for k, ref in enumerate((own_hbm, par_hbm)):
                copy = pltpu.make_async_copy(
                    ref.at[:, which, :, pl.ds(at, width)],
                    kv_ref.at[i, which, :, pl.ds(k * span, span), :],
                    sem.at[len(copies)],
                )
                copy.start()
                copies.append(copy)

    total = ids_ref.shape[1]
    shape = (per, row_dev, total)
    source = lax.broadcasted_iota(jnp.int32, shape, 0) * (2 * row_dev)
    source += core * row_dev + lax.broadcasted_iota(jnp.int32, shape, 1)
    source = source.reshape(rows, total)
    lane = lax.broadcasted_iota(jnp.int32, (rows, total), 1)
    ids = jnp.broadcast_to(ids_ref[...].astype(F32), (rows, total))
    member = jnp.sum(jnp.where(lane == source, ids, 0.0), axis=1, keepdims=True)
    member = jnp.broadcast_to(member, (rows, HD))
    lane = lax.broadcasted_iota(jnp.int32, (rows, HD), 1)
    keep = ((1.0 - member).astype(BF16), member.astype(BF16))

    def scores(i, h):
        q = q_refs[i][h * per : (h + 1) * per].reshape(rows, REP * HD)
        lanes = slice(h * HD, (h + 1) * HD)
        k = jnp.concatenate([kv_ref[i, 0, 0, :, lanes], kv_ref[i, 0, 1, :, lanes]], axis=1)
        tops = []
        half = REP // 2
        for part in range(2):
            block = [q[:, r * HD : (r + 1) * HD] for r in range(part * half, (part + 1) * half)]
            block = [jnp.concatenate([x * keep[0], x * keep[1]], axis=1) for x in block]
            s = _dot_t(jnp.concatenate(block, axis=0), k)
            s_ref[h, part * half * rows : (part + 1) * half * rows] = s
            tops.append(jnp.max(s, axis=1, keepdims=True) * C2)
        return jnp.concatenate(tops, axis=0)

    def attend(i, h, peak):
        w = jnp.exp2(s_ref[h] * C2 - peak)
        totals = jnp.sum(w, axis=1, keepdims=True)
        lanes = slice(h * HD, (h + 1) * HD)
        v = jnp.concatenate([kv_ref[i, 1, 0, :, lanes], kv_ref[i, 1, 1, :, lanes]], axis=1)
        acc = jnp.dot(w.astype(BF16), v, preferred_element_type=F32)
        inverse = 1.0 / totals
        weight = jnp.ones((rows, HD), F32)
        top = jnp.zeros((rows, HD), F32)
        zone = slice(h * per, (h + 1) * per)
        for r in range(REP):
            sl = slice(r * rows, (r + 1) * rows)
            o = jnp.where(member > 0.5, acc[sl, HD:], acc[sl, :HD]) * inverse[sl]
            o = o.astype(BF16).reshape(per, row_dev, HD)
            o_refs[i][zone, :, r * HD : (r + 1) * HD] = o
            weight = jnp.where(lane == r, totals[sl], weight)
            top = jnp.where(lane == r, peak[sl], top)
        stats = _stats(top + jnp.log2(weight))
        o_refs[i][zone, :, REP * HD :] = stats.reshape(per, row_dev, HD)

    for i in range(n):
        for copy in copies[4 * i : 4 * i + 4]:
            copy.wait()
        peaks = [scores(i, h) for h in range(2)]
        for h in range(2):
            attend(i, h, peaks[h])


def _prompt(wanted, ids, qs, own, par):
    n = len(wanted)
    zs, row_dev, width = qs[0].shape
    span = own.shape[2]
    rows = zs // 2 * row_dev
    vmem = pl.BlockSpec(memory_space=pltpu.VMEM)
    hbm = pl.BlockSpec(memory_space=pltpu.HBM)
    anywhere = pl.BlockSpec(memory_space=pl.ANY)
    return pl.pallas_call(
        functools.partial(_prompt_kernel, wanted),
        out_shape=[jax.ShapeDtypeStruct((zs, row_dev, width + HD), BF16)] * n,
        in_specs=[vmem] * (n + 1) + [hbm, anywhere],
        out_specs=[vmem] * n,
        scratch_shapes=[
            pltpu.VMEM((n, 2, 2, 2 * span, 2 * HD), BF16),
            pltpu.VMEM((2, rows * REP, 2 * span), F32),
            pltpu.SemaphoreType.DMA((4 * n,)),
        ],
        compiler_params=pltpu.CompilerParams(vmem_limit_bytes=VMEM_LIMIT),
        cost_estimate=pl.CostEstimate(
            flops=n * 2 * 2 * 2 * rows * REP * 2 * span * 2 * HD,
            bytes_accessed=n * 2 * 2 * 4 * span * HD * 2,
            transcendentals=n * 2 * rows * REP * 2 * span,
        ),
    )(ids, *qs, own, par)


def _lse(x):
    s = x.astype(F32)
    return s + pltpu.roll(s, HD - REP, 1) + pltpu.roll(s, HD - 2 * REP, 1)


def _weights(l2s):
    top = functools.reduce(jnp.maximum, l2s)
    es = [jnp.exp2(l2 - top) for l2 in l2s]
    total = functools.reduce(jnp.add, es)
    return [e / total for e in es], top + jnp.log2(total)


def _merge_kernel(*all_refs):
    *refs, o_ref = all_refs
    lead = o_ref.shape[:2]
    rows = lead[0] * lead[1]
    lane = lax.broadcasted_iota(jnp.int32, (rows, HD), 1)
    l2s = [_lse(ref[:, :, REP * HD :].reshape(rows, HD)) for ref in refs]
    l2s = [jnp.where(lane < REP, x, 0.0) for x in l2s]
    ws, l2 = _weights(l2s)
    for r in range(REP):
        acc = None
        for w, ref in zip(ws, refs):
            x = ref[:, :, r * HD : (r + 1) * HD].reshape(rows, HD).astype(F32)
            x = x * w[:, r : r + 1]
            acc = x if acc is None else acc + x
        o_ref[:, :, r * HD : (r + 1) * HD] = acc.astype(BF16).reshape(*lead, HD)
    o_ref[:, :, REP * HD :] = _stats(l2).reshape(*lead, HD)


def _merge(parts):
    return pl.pallas_call(
        _merge_kernel,
        out_shape=jax.ShapeDtypeStruct(parts[0].shape, BF16),
        compiler_params=pltpu.CompilerParams(vmem_limit_bytes=VMEM_LIMIT),
    )(*parts)


def _final_kernel(p_ref, so_ref, sl_ref, o_ref):
    n = p_ref.shape[0]
    rows = p_ref.shape[1]
    lane = lax.broadcasted_iota(jnp.int32, (rows, HD), 1)
    l2s = [_lse(p_ref[i, :, REP * HD :]) for i in range(n)] + [sl_ref[...]]
    ws, _ = _weights([jnp.where(lane < REP, x, 0.0) for x in l2s])
    for r in range(REP):
        sl = slice(r * HD, (r + 1) * HD)
        acc = so_ref[:, sl] * ws[n][:, r : r + 1]
        for i in range(n):
            acc += p_ref[i, :, sl].astype(F32) * ws[i][:, r : r + 1]
        o_ref[:, sl] = acc.astype(BF16)


def _final(parts, suffix_o, suffix_l2):
    return pl.pallas_call(
        _final_kernel,
        out_shape=jax.ShapeDtypeStruct(suffix_o.shape, BF16),
        compiler_params=pltpu.CompilerParams(vmem_limit_bytes=VMEM_LIMIT),
    )(parts, suffix_o, suffix_l2)


def _suffix(q, kv, lengths):
    rows, suf = kv.shape[0], kv.shape[1]
    own_q = q.reshape(rows, REP, HD)
    scores = jnp.einsum("rhd,rsd->rhs", own_q, kv[:, :, 0], preferred_element_type=F32) * C2
    valid = jnp.arange(suf, dtype=jnp.int32)[None, None, :] < lengths[:, None, None]
    scores = jnp.where(valid, scores, -BIG)
    peak = jnp.max(scores, axis=2, keepdims=True)
    probs = jnp.exp2(scores - peak)
    total = jnp.sum(probs, axis=2)
    numer = jnp.einsum("rhs,rsd->rhd", probs.astype(BF16), kv[:, :, 1], preferred_element_type=F32)
    o = (numer / total[:, :, None]).reshape(rows, REP * HD)
    l2 = jnp.pad(peak[:, :, 0] + jnp.log2(total), ((0, 0), (0, HD - REP)))
    return o, l2


def _pairs(which):
    out = []
    for y in range(4):
        for core in range(2):
            to = 3 - y if (which == 1) == (core == 1) else y ^ 1
            out.append((2 * y + core, 2 * to + core))
    return out


def _shards(queries, prompt_kv, suffix_kv, suffix_len, group_of):
    q = queries[0]
    own = jnp.transpose(prompt_kv[0], (0, 2, 1, 3))

    n_z = lax.axis_size("zh") * lax.axis_size("zl")
    spread = jnp.broadcast_to(q[None], (n_z, *q.shape))
    q0 = lax.all_to_all(spread, ("zh", "zl"), 0, 0, tiled=True)
    suffix_o, suffix_l2 = _suffix(q, suffix_kv[0], suffix_len[0])
    q0, own, suffix_o, suffix_l2 = lax.optimization_barrier((q0, own, suffix_o, suffix_l2))
    par = lax.ppermute(own, "core", [(0, 1), (1, 0)])
    first = lax.ppermute(q0, ("y", "core"), _pairs(1))
    first, q0 = lax.optimization_barrier((first, q0))
    third = lax.ppermute(first, ("y", "core"), _pairs(2))
    second = lax.ppermute(q0, ("y", "core"), _pairs(2))

    def part(which, block):
        return _prompt((which,), group_of, [block], own, par)[0]

    part_first, third = lax.optimization_barrier((part(1, first), third))
    back_third = lax.ppermute(part(3, third), ("y", "core"), _pairs(2))
    back_second = lax.ppermute(part(2, second), ("y", "core"), _pairs(2))
    merged = _merge([part_first, back_third])
    back_first = lax.ppermute(merged, ("y", "core"), _pairs(1))
    merged = _merge([part(0, q0), back_second, back_first])
    got = lax.all_to_all(merged, ("zh", "zl"), 0, 0, tiled=True)
    return _final(got, suffix_o, suffix_l2)[None]


def solution(mesh):
    fine = Mesh(
        np.asarray(mesh.devices).reshape(4, 2, 4, 2, 4), ("y", "zh", "zl", "core", "grp")
    )
    ctx, dec = ("y", "zh"), ("zl", "core")
    placed = (
        P("grp", dec, ctx),
        P("grp", None, ctx + dec, None, None),
        P("grp", dec, None, None, ctx),
        P("grp", dec),
        P("grp", None),
    )
    return jax.shard_map(
        _shards, mesh=fine, in_specs=placed, out_specs=P("grp", dec, ctx), check_vma=False
    )
```
